512 devices in a mesh: peer: 16 (over z_lo, x), zero: 32 (over y, z_hi, core).
Axes of the slice: x: 4, y: 4, z: 16 (z_hi: 4, z_lo: 4; z = z_hi * 4 + z_lo), core: 2. Of those that a mesh axis runs over, the one named last changes fastest.
Arguments:
- step: int32 [1], replicated, may hold values from 0 to 63
- grads: bfloat16 [16, 32, 1, 2, 128, 3584], P('peer', 'zero'), may hold values from -64 to 64
- master: float32 [16, 2, 128, 3584], P('peer', None, 'zero'), may hold values from -4 to 4
- first_moment: float32 [16, 2, 128, 3584], P('peer', None, 'zero'), may hold values from -1.75 to 1.75
- second_moment: float32 [16, 2, 128, 3584], P('peer', None, 'zero'), may hold values from 0.01 to 1
Outputs:
- new_master: float32 [16, 2, 128, 3584], P('peer', None, 'zero')
- new_first: float32 [16, 2, 128, 3584], P('peer', None, 'zero')
- new_second: float32 [16, 2, 128, 3584], P('peer', None, 'zero')
- params_bf16: bfloat16 [16, 2, 128, 3584], P('peer')
The draws below stay inside these ranges and needn't reach their ends.
All inputs are finite; a program needn't handle non-finite values.
Results may differ from the reference program's by a relative error of at most 0.001.
Values may be sent and summed in bfloat16 or wider, within the bound.
No kernel may reach another device: no remote copies, remote signals or barrier semaphores. Data moves between devices by JAX's collectives and lax.ppermute only.
A program may use at most 64 MiB of HBM per device.

```python
import math
import jax
import jax.numpy as jnp
from jax import lax

D = 3584
LAYERS = 2
MICRO = 1
ROWS = 128
GROUPS = 16
N_PEER = 16
N_ZERO = 32


def spiked(result, rng, source, target, blocks, factor):
    def block_of(dim):
        return (jnp.arange(result.shape[dim]) // (result.shape[dim] // blocks)).reshape((-1,) + (1,) * (result.ndim - 1 - dim))

    near = jax.random.permutation(rng, blocks)[block_of(target)]
    far = (block_of(target) + blocks // 2) % blocks
    return jnp.where((block_of(source) == near) | (block_of(source) == far), factor * result, result)


def steps_of(key, shape, pieces, smallest, high):
    def one(axis_at, blocks):
        draws = jax.random.uniform(jax.random.fold_in(jax.random.fold_in(key, 6), axis_at), (blocks,), jnp.float32, smallest / len(pieces), high / len(pieces))
        return jnp.repeat(jnp.exp(draws), shape[axis_at] // blocks).reshape((-1,) + (1,) * (len(shape) - axis_at - 1))

    gain = one(*pieces[0])
    for cut in pieces[1:]:
        gain = gain * one(*cut)
    return gain


def noise(stream_key, extent, width, reach, cuts=(), dtype=jnp.bfloat16):
    drawn = width * jax.random.normal(stream_key, extent, jnp.float32)
    if cuts:
        drawn = drawn * steps_of(stream_key, extent, cuts, -0.22, 0.18)
    return jnp.clip(drawn, -reach, reach).astype(dtype)


def gaussian_with(rng, dims, spread, limit, split, heavy, dtype=jnp.bfloat16):
    values = spread * jax.random.normal(rng, dims, jnp.float32)
    if split:
        values = values * steps_of(rng, dims, split, -0.22, 0.18)
    return jnp.clip(spiked(values, jax.random.fold_in(rng, 3), *heavy), -limit, limit).astype(dtype)


def setup_inputs(seed: int = 0) -> dict:
    key_list = jax.random.split(jax.random.key(seed), 6)
    return {
        "step": jax.random.randint(key_list[0], (1,), 0, 64).astype(jnp.int32),
        "grads": gaussian_with(key_list[1], (GROUPS, N_ZERO, MICRO, LAYERS, ROWS, D), ((N_ZERO * MICRO) ** 0.5), 64.0, ((0, 16), (1, 32)), (1, 4, 32, 2.75)),
        "master": noise(key_list[2], (GROUPS, LAYERS, ROWS, D), 0.3, 4.0, ((0, 16), (2, 32)), jnp.float32),
        "first_moment": noise(key_list[3], (GROUPS, LAYERS, ROWS, D), 0.3, 1.75, ((0, 16), (2, 32)), jnp.float32),
        "second_moment": jnp.clip(jnp.exp(math.log(1.0) - 4.6051702 * jax.random.uniform(key_list[4], (GROUPS, LAYERS, ROWS, D), jnp.float32) ** steps_of(key_list[4], (GROUPS, LAYERS, ROWS, D), ((0, 16), (2, 32)), -0.2, 0.2)), 0.01, 1.0),
    }


def reference(step, grads, master, first_moment, second_moment):
    t = step[0]
    scale = 1.0 / (N_ZERO * MICRO)

    def group_mean(block):
        return lax.optimization_barrier(jnp.sum(block.astype(jnp.float32), axis=(0, 1))) * scale
    mean_grad = lax.map(group_mean, grads)
    new_first = 0.9 * first_moment + 0.1 * mean_grad
    new_second = 0.95 * second_moment + 0.05 * mean_grad * mean_grad
    power = (t + 1).astype(jnp.float32)
    corr_one = 1.0 - jnp.power(jnp.float32(0.9), power)
    corr_two = 1.0 - jnp.power(jnp.float32(0.95), power)
    updated = master - 0.05 * (new_first / corr_one / (jnp.sqrt(new_second / corr_two) + 1e-08) + 0.1 * master)
    which = t % 3
    rolled_one = jnp.roll(updated, 1 % N_PEER, axis=0)
    rolled_two = jnp.roll(updated, 2 % N_PEER, axis=0)
    rolled_four = jnp.roll(updated, 4 % N_PEER, axis=0)
    partner = jnp.where(which == 0, rolled_one, jnp.where(which == 1, rolled_two, rolled_four))
    new_master = (updated + partner) * 0.5
    return (new_master, new_first, new_second, new_master.astype(jnp.bfloat16))
```

```python
import jax
import jax.numpy as jnp
from jax import lax
from jax.sharding import Mesh, PartitionSpec as P

PEER = ("zlo", "x")
ZERO = ("y", "zhi", "core")
F32 = jnp.float32
BF16 = jnp.bfloat16


def shifted(block, axis, distance):
    n = lax.axis_size(axis)
    return lax.ppermute(block, axis, [(i, (i + distance) % n) for i in range(n)])


def piece(stack, index):
    return lax.dynamic_index_in_dim(stack, index, 0, keepdims=False)


def reduce_over(stack, axis):
    n = lax.axis_size(axis)
    me = lax.axis_index(axis)
    total = piece(stack, me)
    for k in (1, n - 1, 2):
        total = total + shifted(piece(stack, (me + k) % n), axis, k)
    return total


def body(step, grads, master, first_moment, second_moment):
    t = step[0]
    power = (t + 1).astype(F32)
    corr_one = 1.0 - jnp.power(F32(0.9), power)
    corr_two = 1.0 - jnp.power(F32(0.95), power)
    depth = master.shape[-1]
    ny, nz, nc = (lax.axis_size(a) for a in ZERO)

    local = grads[0, 0, 0].reshape(2, ny, nz, nc, 4, depth)
    local = local.transpose(3, 1, 2, 0, 4, 5).reshape(nc, ny, nz * 8, depth)
    core = lax.axis_index("core")
    theirs = shifted(piece(local, 1 - core), "core", 1)
    part = piece(local, core).astype(F32) + theirs.astype(F32)
    part = reduce_over(part, "y")
    part = reduce_over(part.reshape(nz, 8, depth), "zhi")
    mean_grad = part.reshape(2, 4, depth) * (1.0 / 32)

    new_first = 0.9 * first_moment[0] + 0.1 * mean_grad
    new_second = 0.95 * second_moment[0] + 0.05 * mean_grad * mean_grad
    updated = master[0] - 0.05 * (
        new_first / corr_one / (jnp.sqrt(new_second / corr_two) + 1e-08) + 0.1 * master[0]
    )
    partner = lax.switch(
        t % 3, [lambda u, d=d: shifted(u, PEER, d) for d in (1, 2, 4)], updated
    )
    averaged = (updated + partner) * 0.5

    whole = averaged.astype(BF16).reshape(8, depth)
    whole = lax.all_gather(whole, "zhi", axis=0)
    whole = lax.all_gather(whole, "y", axis=0)
    other = shifted(whole, "core", 1)
    pair = jnp.where(core == 0, jnp.stack([whole, other]), jnp.stack([other, whole]))
    pair = pair.reshape(nc, ny, nz, 2, 4, depth).transpose(3, 1, 2, 0, 4, 5)
    whole = pair.reshape(2, ny * nz * nc * 4, depth)
    return (averaged[None], new_first[None], new_second[None], whole[None])


def solution(mesh):
    fine = Mesh(mesh.devices.reshape(4, 4, 4, 4, 2), PEER + ZERO)
    shard = P(PEER, None, ZERO, None)
    return jax.shard_map(
        body,
        mesh=fine,
        in_specs=(P(), P(PEER, ZERO, None, None, None, None), shard, shard, shard),
        out_specs=(shard, shard, shard, P(PEER, None, None, None)),
        check_vma=False,
    )
```

```python
import jax
import jax.numpy as jnp
from jax import lax
from jax.experimental import pallas as pl
from jax.experimental.pallas import tpu as pltpu
from jax.sharding import Mesh, PartitionSpec as P

PEER = ("zlo", "x")
ZERO = ("y", "zhi", "core")
F32 = jnp.float32
BF16 = jnp.bfloat16
VMEM = pl.BlockSpec(memory_space=pltpu.VMEM)
SMEM = pl.BlockSpec(memory_space=pltpu.SMEM)
LANES = 512
PARAMS = pltpu.CompilerParams(vmem_limit_bytes=32 * 2**20)


def shifted(block, axis, distance):
    n = lax.axis_size(axis)
    return lax.ppermute(block, axis, [(i, (i + distance) % n) for i in range(n)])


def low_high(a, b):
    row = lax.broadcasted_iota(jnp.int32, a.shape, 0)
    low = jnp.where(row < 4, a, pltpu.roll(b, 4, 0))
    high = jnp.where(row < 4, pltpu.roll(a, 4, 0), b)
    return low, high


def split_kernel(where_ref, grads_ref, mine_ref, theirs_ref):
    first = where_ref[1] == 0
    depth = grads_ref.shape[-1]
    for at in range(0, depth, LANES):
        cols = slice(at, at + LANES)
        a = grads_ref[0, :, cols].astype(F32)
        b = grads_ref[1, :, cols].astype(F32)
        mine, theirs = [], []
        for r in range(0, a.shape[0], 8):
            low, high = low_high(a[r : r + 8], b[r : r + 8])
            mine.append(jnp.where(first, low, high))
            theirs.append(jnp.where(first, high, low))
        mine_ref[0, :, cols] = jnp.concatenate(mine, 0).astype(BF16)
        theirs_ref[0, :, cols] = jnp.concatenate(theirs, 0).astype(BF16)


def split_cores(grads, y, core):
    layers, rows, depth = grads.shape
    ny = lax.axis_size("y")
    per = rows // ny
    out = jax.ShapeDtypeStruct((ny, per, depth), BF16)
    block = pl.BlockSpec((1, per, depth), lambda k, w: (k, 0, 0))
    return pl.pallas_call(
        split_kernel,
        grid_spec=pltpu.PrefetchScalarGridSpec(
            num_scalar_prefetch=1,
            grid=(ny,),
            in_specs=[pl.BlockSpec((layers, per, depth), lambda k, w: (0, (w[0] + k) % ny, 0))],
            out_specs=[block, block],
        ),
        out_shape=(out, out),
        compiler_params=PARAMS,
        name="split_cores",
    )(jnp.stack([y, core]).astype(jnp.int32), grads)


def add_pair_kernel(mine_ref, theirs_ref, *outs):
    for k, out in enumerate(outs):
        out[...] = mine_ref[k].astype(F32) + theirs_ref[k].astype(F32)


def add_pair(mine, theirs):
    n, rows, depth = mine.shape
    out = jax.ShapeDtypeStruct((rows, depth), F32)
    return pl.pallas_call(
        add_pair_kernel,
        in_specs=[VMEM, VMEM],
        out_specs=[VMEM] * n,
        out_shape=[out] * n,
        compiler_params=PARAMS,
        name="add_pair",
    )(mine, theirs)


def add_four_kernel(z_ref, a_ref, b_ref, c_ref, d_ref, *outs):
    n = len(outs)
    for k, out in enumerate(outs):
        at = pl.ds(pl.multiple_of(((z_ref[0] + k) % n) * 8, 8), 8)
        out[...] = (a_ref[at, :] + b_ref[at, :]) + (c_ref[at, :] + d_ref[at, :])


def add_four(z, parts):
    rows, depth = parts[0].shape
    n = rows // 8
    out = jax.ShapeDtypeStruct((8, depth), F32)
    return pl.pallas_call(
        add_four_kernel,
        in_specs=[SMEM] + [VMEM] * 4,
        out_specs=[VMEM] * n,
        out_shape=[out] * n,
        compiler_params=PARAMS,
        name="add_four",
    )(z.astype(jnp.int32)[None], *parts)


def adam_kernel(corr_ref, a_ref, b_ref, c_ref, d_ref, master_ref, first_ref, second_ref, nf_ref, ns_ref, up_ref):
    mean_all = ((a_ref[...] + b_ref[...]) + (c_ref[...] + d_ref[...])) * (1.0 / 32)
    for layer in range(2):
        mean = mean_all[4 * layer : 4 * layer + 4]
        master = master_ref[layer]
        nf = 0.9 * first_ref[layer] + 0.1 * mean
        ns = 0.95 * second_ref[layer] + 0.05 * mean * mean
        nf_ref[layer] = nf
        ns_ref[layer] = ns
        up_ref[layer] = master - 0.05 * (
            nf / corr_ref[0] / (jnp.sqrt(ns / corr_ref[1]) + 1e-08) + 0.1 * master
        )


def adam(corr, parts, master, first, second):
    out = jax.ShapeDtypeStruct(master.shape, F32)
    return pl.pallas_call(
        adam_kernel,
        in_specs=[SMEM] + [VMEM] * 7,
        out_specs=[VMEM] * 3,
        out_shape=[out] * 3,
        compiler_params=PARAMS,
        name="adam",
    )(corr, *parts, master, first, second)


def join_kernel(core_ref, mine_ref, theirs_ref, out_ref):
    first = core_ref[0] == 0
    depth = mine_ref.shape[-1]
    for at in range(0, depth, LANES):
        cols = slice(at, at + LANES)
        mine = mine_ref[:, cols].astype(F32)
        theirs = theirs_ref[:, cols].astype(F32)
        a = jnp.where(first, mine, theirs)
        b = jnp.where(first, theirs, mine)
        lows, highs = [], []
        for r in range(0, a.shape[0], 8):
            low, high = low_high(a[r : r + 8], b[r : r + 8])
            lows.append(low)
            highs.append(high)
        out_ref[0, :, cols] = jnp.concatenate(lows, 0).astype(BF16)
        out_ref[1, :, cols] = jnp.concatenate(highs, 0).astype(BF16)


def join_cores(mine, theirs, core):
    rows, depth = mine.shape
    steps = 4
    per = rows // steps
    block = pl.BlockSpec((per, depth), lambda k, w: (k, 0))
    return pl.pallas_call(
        join_kernel,
        grid_spec=pltpu.PrefetchScalarGridSpec(
            num_scalar_prefetch=1,
            grid=(steps,),
            in_specs=[block, block],
            out_specs=pl.BlockSpec((2, per, depth), lambda k, w: (0, k, 0)),
        ),
        out_shape=jax.ShapeDtypeStruct((2, rows, depth), BF16),
        compiler_params=PARAMS,
        name="join_cores",
    )(core.astype(jnp.int32)[None], mine, theirs)


def body(step, grads, master, first_moment, second_moment):
    t = step[0]
    power = (t + 1).astype(F32)
    corr = jnp.stack([1.0 - jnp.power(F32(0.9), power), 1.0 - jnp.power(F32(0.95), power)])
    depth = master.shape[-1]
    y, z, core = (lax.axis_index(a) for a in ZERO)

    mine, theirs = split_cores(grads[0, 0, 0], y, core)
    parts = add_pair(mine, shifted(theirs, "core", 1))
    two = shifted(parts[2], "y", 2)
    parts = [parts[0], shifted(parts[1], "y", 1), two, shifted(parts[3], "y", 3)]
    parts = add_four(z, parts)
    two = shifted(parts[2], "zhi", 2)
    parts = [parts[0], shifted(parts[1], "zhi", 1), two, shifted(parts[3], "zhi", 3)]
    new_first, new_second, updated = adam(
        corr, parts, master[0], first_moment[0], second_moment[0]
    )
    partner = lax.switch(
        t % 3, [lambda u, d=d: shifted(u, PEER, d) for d in (1, 2, 4)], updated
    )
    averaged = (updated + partner) * 0.5

    whole = averaged.astype(BF16).reshape(8, depth)
    whole = lax.all_gather(whole, "zhi", axis=0, tiled=True)
    whole = lax.all_gather(whole, "y", axis=0, tiled=True)
    whole = join_cores(whole, shifted(whole, "core", 1), core)
    return (averaged[None], new_first[None], new_second[None], whole[None])


def solution(mesh):
    fine = Mesh(mesh.devices.reshape(4, 4, 4, 4, 2), PEER + ZERO)
    shard = P(PEER, None, ZERO, None)
    return jax.shard_map(
        body,
        mesh=fine,
        in_specs=(P(), P(PEER, ZERO, None, None, None, None), shard, shard, shard),
        out_specs=(shard, shard, shard, P(PEER, None, None, None)),
        check_vma=False,
    )
```

```python
import jax
import jax.numpy as jnp
from jax import lax
from jax.experimental import pallas as pl
from jax.experimental.pallas import tpu as pltpu
from jax.sharding import Mesh, PartitionSpec as P

PEER = ("zlo", "x")
ZERO = ("y", "zhi", "core")
F32 = jnp.float32
BF16 = jnp.bfloat16
VMEM = pl.BlockSpec(memory_space=pltpu.VMEM)
SMEM = pl.BlockSpec(memory_space=pltpu.SMEM)
LANES = 512
PARAMS = pltpu.CompilerParams(vmem_limit_bytes=32 * 2**20)


def shifted(block, axis, distance):
    n = lax.axis_size(axis)
    return lax.ppermute(block, axis, [(i, (i + distance) % n) for i in range(n)])


def turned(block, distance):
    n = lax.axis_size("zhi")
    pairs = []
    for z in range(n):
        pairs.append((2 * z, 2 * ((z + distance) % n)))
        pairs.append((2 * z + 1, 2 * ((z - distance) % n) + 1))
    return lax.ppermute(block, ("zhi", "core"), pairs)


def low_high(a, b):
    row = lax.broadcasted_iota(jnp.int32, a.shape, 0)
    low = jnp.where(row < 4, a, pltpu.roll(b, 4, 0))
    high = jnp.where(row < 4, pltpu.roll(a, 4, 0), b)
    return low, high


def split_kernel(where_ref, grads_ref, mine_ref, theirs_ref):
    first = where_ref[1] == 0
    depth = grads_ref.shape[-1]
    for at in range(0, depth, LANES):
        cols = slice(at, at + LANES)
        a = grads_ref[0, :, cols].astype(F32)
        b = grads_ref[1, :, cols].astype(F32)
        mine, theirs = [], []
        for r in range(0, a.shape[0], 8):
            low, high = low_high(a[r : r + 8], b[r : r + 8])
            mine.append(jnp.where(first, low, high))
            theirs.append(jnp.where(first, high, low))
        mine_ref[0, :, cols] = jnp.concatenate(mine, 0).astype(BF16)
        theirs_ref[0, :, cols] = jnp.concatenate(theirs, 0).astype(BF16)


def split_cores(grads, y, core):
    layers, rows, depth = grads.shape
    ny = lax.axis_size("y")
    per = rows // ny
    out = jax.ShapeDtypeStruct((ny, per, depth), BF16)
    block = pl.BlockSpec((1, per, depth), lambda k, w: (k, 0, 0))
    return pl.pallas_call(
        split_kernel,
        grid_spec=pltpu.PrefetchScalarGridSpec(
            num_scalar_prefetch=1,
            grid=(ny,),
            in_specs=[pl.BlockSpec((layers, per, depth), lambda k, w: (0, (w[0] + k) % ny, 0))],
            out_specs=[block, block],
        ),
        out_shape=(out, out),
        compiler_params=PARAMS,
        name="split_cores",
    )(jnp.stack([y, core]).astype(jnp.int32), grads)


def add_pair_kernel(mine_ref, theirs_ref, *outs):
    for k, out in enumerate(outs):
        out[...] = mine_ref[k].astype(F32) + theirs_ref[k].astype(F32)


def add_pair(mine, theirs):
    n, rows, depth = mine.shape
    out = jax.ShapeDtypeStruct((rows, depth), F32)
    return pl.pallas_call(
        add_pair_kernel,
        in_specs=[VMEM, VMEM],
        out_specs=[VMEM] * n,
        out_shape=[out] * n,
        compiler_params=PARAMS,
        name="add_pair",
    )(mine, theirs)


def add_four_kernel(z_ref, a_ref, b_ref, c_ref, d_ref, *outs):
    n = len(outs)
    for k, out in enumerate(outs):
        step = jnp.where(z_ref[1] == 0, k, n - k)
        at = pl.ds(pl.multiple_of(((z_ref[0] + step) % n) * 8, 8), 8)
        out[...] = (a_ref[at, :] + b_ref[at, :]) + (c_ref[at, :] + d_ref[at, :])


def add_four(z, core, parts):
    rows, depth = parts[0].shape
    n = rows // 8
    out = jax.ShapeDtypeStruct((8, depth), F32)
    return pl.pallas_call(
        add_four_kernel,
        in_specs=[SMEM] + [VMEM] * 4,
        out_specs=[VMEM] * n,
        out_shape=[out] * n,
        compiler_params=PARAMS,
        name="add_four",
    )(jnp.stack([z, core]).astype(jnp.int32), *parts)


def adam_kernel(corr_ref, a_ref, b_ref, c_ref, master_ref, first_ref, second_ref, nf_ref, ns_ref, up_ref):
    mean_all = (a_ref[...] + (b_ref[...] + c_ref[...])) * (1.0 / 32)
    for layer in range(2):
        mean = mean_all[4 * layer : 4 * layer + 4]
        master = master_ref[layer]
        nf = 0.9 * first_ref[layer] + 0.1 * mean
        ns = 0.95 * second_ref[layer] + 0.05 * mean * mean
        nf_ref[layer] = nf
        ns_ref[layer] = ns
        up_ref[layer] = master - 0.05 * (
            nf / corr_ref[0] / (jnp.sqrt(ns / corr_ref[1]) + 1e-08) + 0.1 * master
        )


def adam(corr, parts, master, first, second):
    out = jax.ShapeDtypeStruct(master.shape, F32)
    return pl.pallas_call(
        adam_kernel,
        in_specs=[SMEM] + [VMEM] * 6,
        out_specs=[VMEM] * 3,
        out_shape=[out] * 3,
        compiler_params=PARAMS,
        name="adam",
    )(corr, *parts, master, first, second)


def join_kernel(core_ref, mine_ref, theirs_ref, out_ref):
    first = core_ref[0] == 0
    depth = mine_ref.shape[-1]
    for at in range(0, depth, LANES):
        cols = slice(at, at + LANES)
        mine = mine_ref[:, cols].astype(F32)
        theirs = theirs_ref[:, cols].astype(F32)
        a = jnp.where(first, mine, theirs)
        b = jnp.where(first, theirs, mine)
        lows, highs = [], []
        for r in range(0, a.shape[0], 8):
            low, high = low_high(a[r : r + 8], b[r : r + 8])
            lows.append(low)
            highs.append(high)
        out_ref[0, :, cols] = jnp.concatenate(lows, 0).astype(BF16)
        out_ref[1, :, cols] = jnp.concatenate(highs, 0).astype(BF16)


def join_cores(mine, theirs, core):
    rows, depth = mine.shape
    steps = 4
    per = rows // steps
    block = pl.BlockSpec((per, depth), lambda k, w: (k, 0))
    return pl.pallas_call(
        join_kernel,
        grid_spec=pltpu.PrefetchScalarGridSpec(
            num_scalar_prefetch=1,
            grid=(steps,),
            in_specs=[block, block],
            out_specs=pl.BlockSpec((2, per, depth), lambda k, w: (0, k, 0)),
        ),
        out_shape=jax.ShapeDtypeStruct((2, rows, depth), BF16),
        compiler_params=PARAMS,
        name="join_cores",
    )(core.astype(jnp.int32)[None], mine, theirs)


def body(step, grads, master, first_moment, second_moment):
    t = step[0]
    power = (t + 1).astype(F32)
    corr = jnp.stack([1.0 - jnp.power(F32(0.9), power), 1.0 - jnp.power(F32(0.95), power)])
    depth = master.shape[-1]
    y, z, core = (lax.axis_index(a) for a in ZERO)

    mine, theirs = split_cores(grads[0, 0, 0], y, core)
    parts = add_pair(mine, shifted(theirs, "core", 1))
    one, three, two = (shifted(parts[k], "y", k) for k in (1, 3, 2))
    own, near, far, back = add_four(z, core, [one, three, two, parts[0]])
    through = turned(far, 1)
    back = turned(back, -1)
    near = turned(near + through, 1)
    parts = [own, back, near]
    new_first, new_second, updated = adam(
        corr, parts, master[0], first_moment[0], second_moment[0]
    )
    partner = lax.switch(
        t % 3, [lambda u, d=d: shifted(u, PEER, d) for d in (1, 2, 4)], updated
    )
    averaged = (updated + partner) * 0.5

    whole = averaged.astype(BF16).reshape(8, depth)
    whole = lax.all_gather(whole, "zhi", axis=0, tiled=True)
    whole = lax.all_gather(whole, "y", axis=0, tiled=True)
    whole = join_cores(whole, shifted(whole, "core", 1), core)
    return (averaged[None], new_first[None], new_second[None], whole[None])


def solution(mesh):
    fine = Mesh(mesh.devices.reshape(4, 4, 4, 4, 2), PEER + ZERO)
    shard = P(PEER, None, ZERO, None)
    return jax.shard_map(
        body,
        mesh=fine,
        in_specs=(P(), P(PEER, ZERO, None, None, None, None), shard, shard, shard),
        out_specs=(shard, shard, shard, P(PEER, None, None, None)),
        check_vma=False,
    )
```

```python
import jax
import jax.numpy as jnp
from jax import lax
from jax.experimental import pallas as pl
from jax.experimental.pallas import tpu as pltpu
from jax.sharding import Mesh, PartitionSpec as P

PEER = ("zlo", "x")
ZERO = ("y", "zhi", "core")
F32 = jnp.float32
BF16 = jnp.bfloat16
VMEM = pl.BlockSpec(memory_space=pltpu.VMEM)
SMEM = pl.BlockSpec(memory_space=pltpu.SMEM)
LANES = 512
PARAMS = pltpu.CompilerParams(vmem_limit_bytes=32 * 2**20)


def shifted(block, axis, distance):
    n = lax.axis_size(axis)
    return lax.ppermute(block, axis, [(i, (i + distance) % n) for i in range(n)])


def low_high(a, b):
    row = lax.broadcasted_iota(jnp.int32, a.shape, 0)
    low = jnp.where(row < 4, a, pltpu.roll(b, 4, 0))
    high = jnp.where(row < 4, pltpu.roll(a, 4, 0), b)
    return low, high


def split_kernel(core_ref, grads_ref, mine_ref, theirs_ref):
    first = core_ref[0] == 0
    depth = grads_ref.shape[-1]
    for at in range(0, depth, LANES):
        cols = slice(at, at + LANES)
        a = grads_ref[0, :, cols].astype(F32)
        b = grads_ref[1, :, cols].astype(F32)
        mine, theirs = [], []
        for r in range(0, a.shape[0], 8):
            low, high = low_high(a[r : r + 8], b[r : r + 8])
            mine.append(jnp.where(first, low, high))
            theirs.append(jnp.where(first, high, low))
        mine_ref[0, :, cols] = jnp.concatenate(mine, 0).astype(BF16)
        theirs_ref[0, :, cols] = jnp.concatenate(theirs, 0).astype(BF16)


def split_cores(grads, core):
    layers, rows, depth = grads.shape
    ny = lax.axis_size("y")
    per = rows // ny
    out = jax.ShapeDtypeStruct((ny, per, depth), BF16)
    block = pl.BlockSpec((1, per, depth), lambda k, w: (k, 0, 0))
    return pl.pallas_call(
        split_kernel,
        grid_spec=pltpu.PrefetchScalarGridSpec(
            num_scalar_prefetch=1,
            grid=(ny,),
            in_specs=[pl.BlockSpec((layers, per, depth), lambda k, w: (0, k, 0))],
            out_specs=[block, block],
        ),
        out_shape=(out, out),
        compiler_params=PARAMS,
        name="split_cores",
    )(core.astype(jnp.int32)[None], grads)


def scale_of(largest):
    exponent = 14.0 - jnp.floor(jnp.log2(jnp.maximum(largest, 1e-30)))
    return jnp.exp2(exponent), -exponent


def send_scaled(out_ref, sums):
    n, per, _ = out_ref.shape
    depth = sums.shape[-1]
    largest = jnp.zeros((8, LANES), F32)
    for at in range(0, depth, LANES):
        for r in range(0, n * per, 8):
            largest = jnp.maximum(largest, jnp.abs(sums[r : r + 8, at : at + LANES]))
    scale, back = scale_of(jnp.max(largest, axis=(0, 1), keepdims=True))
    for k in range(n):
        for at in range(0, depth, LANES):
            cols = slice(at, at + LANES)
            out_ref[k, :, cols] = sums[k * per : (k + 1) * per, cols] * scale
        out_ref[k, :, depth:] = jnp.broadcast_to(back, (per, out_ref.shape[-1] - depth))


def add_received(total, got_ref, me, cols, depth):
    for k in range(got_ref.shape[0]):
        undo = jnp.exp2(got_ref[k, 0:1, depth : depth + 1])
        total = total + jnp.where(me == k, 0.0, got_ref[k, :, cols] * undo)
    return total


def add_pair_kernel(y_ref, mine_ref, theirs_ref, own_ref, out_ref, sums):
    n, per, depth = mine_ref.shape
    for k in range(n):
        for at in range(0, depth, LANES):
            cols = slice(at, at + LANES)
            sums[k * per : (k + 1) * per, cols] = mine_ref[k, :, cols].astype(F32) + theirs_ref[
                k, :, cols
            ].astype(F32)
    own_ref[...] = sums[pl.ds(pl.multiple_of(y_ref[0] * per, per), per), :]
    send_scaled(out_ref, sums)


def add_pair(y, mine, theirs):
    n, rows, depth = mine.shape
    return pl.pallas_call(
        add_pair_kernel,
        in_specs=[SMEM, VMEM, VMEM],
        out_specs=[VMEM] * 2,
        out_shape=[
            jax.ShapeDtypeStruct((rows, depth), F32),
            jax.ShapeDtypeStruct((n, rows, depth + 128), F32),
        ],
        scratch_shapes=[pltpu.VMEM((n * rows, depth), F32)],
        compiler_params=PARAMS,
        name="add_pair",
    )(y.astype(jnp.int32)[None], mine, theirs)


def add_y_kernel(at_ref, own_ref, got_ref, keep_ref, out_ref, sums):
    depth = own_ref.shape[-1]
    for at in range(0, depth, LANES):
        cols = slice(at, at + LANES)
        sums[:, cols] = add_received(own_ref[:, cols], got_ref, at_ref[0], cols, depth)
    keep_ref[...] = sums[pl.ds(pl.multiple_of(at_ref[1] * 8, 8), 8), :]
    send_scaled(out_ref, sums)


def add_y(y, z, own, got):
    rows, depth = own.shape
    return pl.pallas_call(
        add_y_kernel,
        in_specs=[SMEM, VMEM, VMEM],
        out_specs=[VMEM] * 2,
        out_shape=[
            jax.ShapeDtypeStruct((8, depth), F32),
            jax.ShapeDtypeStruct((rows // 8, 8, depth + 128), F32),
        ],
        scratch_shapes=[pltpu.VMEM((rows, depth), F32)],
        compiler_params=PARAMS,
        name="add_y",
    )(jnp.stack([y, z]).astype(jnp.int32), own, got)


def exchanged(blocks, axis):
    got = lax.all_to_all(blocks.astype(jnp.float16), axis, 0, 0, tiled=True)
    return got.astype(F32)


def adam_kernel(z_ref, corr_ref, own_ref, got_ref, master_ref, first_ref, second_ref, nf_ref, ns_ref, up_ref):
    depth = own_ref.shape[-1]
    total = add_received(own_ref[...], got_ref, z_ref[0], slice(0, depth), depth)
    mean_all = total * (1.0 / 32)
    for layer in range(2):
        mean = mean_all[4 * layer : 4 * layer + 4]
        master = master_ref[layer]
        nf = 0.9 * first_ref[layer] + 0.1 * mean
        ns = 0.95 * second_ref[layer] + 0.05 * mean * mean
        nf_ref[layer] = nf
        ns_ref[layer] = ns
        up_ref[layer] = master - 0.05 * (
            nf / corr_ref[0] / (jnp.sqrt(ns / corr_ref[1]) + 1e-08) + 0.1 * master
        )


def adam(z, corr, own, got, master, first, second):
    out = jax.ShapeDtypeStruct(master.shape, F32)
    return pl.pallas_call(
        adam_kernel,
        in_specs=[SMEM] * 2 + [VMEM] * 5,
        out_specs=[VMEM] * 3,
        out_shape=[out] * 3,
        compiler_params=PARAMS,
        name="adam",
    )(z.astype(jnp.int32)[None], corr, own, got, master, first, second)


def join_kernel(core_ref, mine_ref, theirs_ref, out_ref):
    first = core_ref[0] == 0
    depth = mine_ref.shape[-1]
    for at in range(0, depth, LANES):
        cols = slice(at, at + LANES)
        mine = mine_ref[:, cols].astype(F32)
        theirs = theirs_ref[:, cols].astype(F32)
        a = jnp.where(first, mine, theirs)
        b = jnp.where(first, theirs, mine)
        lows, highs = [], []
        for r in range(0, a.shape[0], 8):
            low, high = low_high(a[r : r + 8], b[r : r + 8])
            lows.append(low)
            highs.append(high)
        out_ref[0, :, cols] = jnp.concatenate(lows, 0).astype(BF16)
        out_ref[1, :, cols] = jnp.concatenate(highs, 0).astype(BF16)


def join_cores(mine, theirs, core):
    rows, depth = mine.shape
    steps = 4
    per = rows // steps
    block = pl.BlockSpec((per, depth), lambda k, w: (k, 0))
    return pl.pallas_call(
        join_kernel,
        grid_spec=pltpu.PrefetchScalarGridSpec(
            num_scalar_prefetch=1,
            grid=(steps,),
            in_specs=[block, block],
            out_specs=pl.BlockSpec((2, per, depth), lambda k, w: (0, k, 0)),
        ),
        out_shape=jax.ShapeDtypeStruct((2, rows, depth), BF16),
        compiler_params=PARAMS,
        name="join_cores",
    )(core.astype(jnp.int32)[None], mine, theirs)


def body(step, grads, master, first_moment, second_moment):
    t = step[0]
    power = (t + 1).astype(F32)
    corr = jnp.stack([1.0 - jnp.power(F32(0.9), power), 1.0 - jnp.power(F32(0.95), power)])
    depth = master.shape[-1]
    y, z, core = (lax.axis_index(a) for a in ZERO)

    mine, theirs = split_cores(grads[0, 0, 0], core)
    own, out = add_pair(y, mine, shifted(theirs, "core", 1))
    own, out = add_y(y, z, own, exchanged(out, "y"))
    new_first, new_second, updated = adam(
        z, corr, own, exchanged(out, "zhi"), master[0], first_moment[0], second_moment[0]
    )
    partner = lax.switch(
        t % 3, [lambda u, d=d: shifted(u, PEER, d) for d in (1, 2, 4)], updated
    )
    averaged = (updated + partner) * 0.5

    whole = averaged.astype(BF16).reshape(8, depth)
    whole = lax.all_gather(whole, "zhi", axis=0, tiled=True)
    whole = lax.all_gather(whole, "y", axis=0, tiled=True)
    whole = join_cores(whole, shifted(whole, "core", 1), core)
    return (averaged[None], new_first[None], new_second[None], whole[None])


def solution(mesh):
    fine = Mesh(mesh.devices.reshape(4, 4, 4, 4, 2), PEER + ZERO)
    shard = P(PEER, None, ZERO, None)
    return jax.shard_map(
        body,
        mesh=fine,
        in_specs=(P(), P(PEER, ZERO, None, None, None, None), shard, shard, shard),
        out_specs=(shard, shard, shard, P(PEER, None, None, None)),
        check_vma=False,
    )
```

```python
import jax
import jax.numpy as jnp
from jax import lax
from jax.experimental import pallas as pl
from jax.experimental.pallas import tpu as pltpu
from jax.sharding import Mesh, PartitionSpec as P

PEER = ("zlo", "x")
ZERO = ("y", "zhi", "core")
F32 = jnp.float32
BF16 = jnp.bfloat16
VMEM = pl.BlockSpec(memory_space=pltpu.VMEM)
SMEM = pl.BlockSpec(memory_space=pltpu.SMEM)
LANES = 512
PARAMS = pltpu.CompilerParams(vmem_limit_bytes=32 * 2**20)


def shifted(block, axis, distance):
    n = lax.axis_size(axis)
    return lax.ppermute(block, axis, [(i, (i + distance) % n) for i in range(n)])


def low_high(a, b):
    row = lax.broadcasted_iota(jnp.int32, a.shape, 0)
    low = jnp.where(row < 4, a, pltpu.roll(b, 4, 0))
    high = jnp.where(row < 4, pltpu.roll(a, 4, 0), b)
    return low, high


def split_kernel(core_ref, grads_ref, mine_ref, theirs_ref):
    first = core_ref[0] == 0
    depth = grads_ref.shape[-1]
    for at in range(0, depth, LANES):
        cols = slice(at, at + LANES)
        a = grads_ref[0, :, cols].astype(F32)
        b = grads_ref[1, :, cols].astype(F32)
        mine, theirs = [], []
        for r in range(0, a.shape[0], 8):
            low, high = low_high(a[r : r + 8], b[r : r + 8])
            mine.append(jnp.where(first, low, high))
            theirs.append(jnp.where(first, high, low))
        mine_ref[0, :, cols] = jnp.concatenate(mine, 0).astype(BF16)
        theirs_ref[0, :, cols] = jnp.concatenate(theirs, 0).astype(BF16)


def split_cores(grads, core):
    layers, rows, depth = grads.shape
    ny = lax.axis_size("y")
    per = rows // ny
    out = jax.ShapeDtypeStruct((ny, per, depth), BF16)
    block = pl.BlockSpec((1, per, depth), lambda k, w: (k, 0, 0))
    return pl.pallas_call(
        split_kernel,
        grid_spec=pltpu.PrefetchScalarGridSpec(
            num_scalar_prefetch=1,
            grid=(ny,),
            in_specs=[pl.BlockSpec((layers, per, depth), lambda k, w: (0, k, 0))],
            out_specs=[block, block],
        ),
        out_shape=(out, out),
        compiler_params=PARAMS,
        name="split_cores",
    )(core, grads)


def scale_of(largest):
    exponent = 14.0 - jnp.floor(jnp.log2(jnp.maximum(largest, 1e-30)))
    return jnp.exp2(exponent), -exponent


def send_scaled(out_ref, sums):
    n, per, _ = out_ref.shape
    depth = sums.shape[-1]
    largest = jnp.zeros((8, LANES), F32)
    for at in range(0, depth, LANES):
        for r in range(0, n * per, 8):
            largest = jnp.maximum(largest, jnp.abs(sums[r : r + 8, at : at + LANES]))
    scale, back = scale_of(jnp.max(largest, axis=(0, 1), keepdims=True))
    for k in range(n):
        for at in range(0, depth, LANES):
            cols = slice(at, at + LANES)
            out_ref[k, :, cols] = sums[k * per : (k + 1) * per, cols] * scale
        out_ref[k, :, depth:] = jnp.broadcast_to(back, (per, out_ref.shape[-1] - depth))


def add_received(total, got_ref, me, cols, depth):
    for k in range(got_ref.shape[0]):
        undo = jnp.exp2(got_ref[k, 0:1, depth : depth + 1])
        total = total + jnp.where(me == k, 0.0, got_ref[k, :, cols] * undo)
    return total


def add_pair_kernel(y_ref, mine_ref, theirs_ref, own_ref, out_ref, sums):
    n, per, depth = mine_ref.shape
    for k in range(n):
        for at in range(0, depth, LANES):
            cols = slice(at, at + LANES)
            sums[k * per : (k + 1) * per, cols] = mine_ref[k, :, cols].astype(F32) + theirs_ref[
                k, :, cols
            ].astype(F32)
    own_ref[...] = sums[pl.ds(pl.multiple_of(y_ref[0] * per, per), per), :]
    send_scaled(out_ref, sums)


def add_pair(y, mine, theirs):
    n, rows, depth = mine.shape
    return pl.pallas_call(
        add_pair_kernel,
        in_specs=[SMEM, VMEM, VMEM],
        out_specs=[VMEM] * 2,
        out_shape=[
            jax.ShapeDtypeStruct((rows, depth), F32),
            jax.ShapeDtypeStruct((n, rows, depth + 128), F32),
        ],
        scratch_shapes=[pltpu.VMEM((n * rows, depth), F32)],
        compiler_params=PARAMS,
        name="add_pair",
    )(y, mine, theirs)


def add_y_kernel(at_ref, own_ref, got_ref, keep_ref, out_ref, sums):
    depth = own_ref.shape[-1]
    for at in range(0, depth, LANES):
        cols = slice(at, at + LANES)
        sums[:, cols] = add_received(own_ref[:, cols], got_ref, at_ref[0], cols, depth)
    keep_ref[...] = sums[pl.ds(pl.multiple_of(at_ref[1] * 8, 8), 8), :]
    send_scaled(out_ref, sums)


def add_y(at, own, got):
    rows, depth = own.shape
    return pl.pallas_call(
        add_y_kernel,
        in_specs=[SMEM, VMEM, VMEM],
        out_specs=[VMEM] * 2,
        out_shape=[
            jax.ShapeDtypeStruct((8, depth), F32),
            jax.ShapeDtypeStruct((rows // 8, 8, depth + 128), F32),
        ],
        scratch_shapes=[pltpu.VMEM((rows, depth), F32)],
        compiler_params=PARAMS,
        name="add_y",
    )(at, own, got)


def exchanged(blocks, axis):
    got = lax.all_to_all(blocks.astype(jnp.float16), axis, 0, 0, tiled=True)
    return got.astype(F32)


def adam_kernel(z_ref, corr_ref, own_ref, got_ref, master_ref, first_ref, second_ref, nf_ref, ns_ref, up_ref):
    depth = own_ref.shape[-1]
    total = add_received(own_ref[...], got_ref, z_ref[0], slice(0, depth), depth)
    mean_all = total * (1.0 / 32)
    for layer in range(2):
        mean = mean_all[4 * layer : 4 * layer + 4]
        master = master_ref[layer]
        nf = 0.9 * first_ref[layer] + 0.1 * mean
        ns = 0.95 * second_ref[layer] + 0.05 * mean * mean
        nf_ref[layer] = nf
        ns_ref[layer] = ns
        up_ref[layer] = master - 0.05 * (
            nf / corr_ref[0] / (jnp.sqrt(ns / corr_ref[1]) + 1e-08) + 0.1 * master
        )


def adam(z, corr, own, got, master, first, second):
    out = jax.ShapeDtypeStruct(master.shape, F32)
    return pl.pallas_call(
        adam_kernel,
        in_specs=[SMEM] * 2 + [VMEM] * 5,
        out_specs=[VMEM] * 3,
        out_shape=[out] * 3,
        compiler_params=PARAMS,
        name="adam",
    )(z, corr, own, got, master, first, second)


def join_kernel(core_ref, mine_ref, theirs_ref, out_ref):
    first = core_ref[0] == 0
    depth = mine_ref.shape[-1]
    for at in range(0, depth, LANES):
        cols = slice(at, at + LANES)
        mine = mine_ref[:, cols].astype(F32)
        theirs = theirs_ref[:, cols].astype(F32)
        a = jnp.where(first, mine, theirs)
        b = jnp.where(first, theirs, mine)
        lows, highs = [], []
        for r in range(0, a.shape[0], 8):
            low, high = low_high(a[r : r + 8], b[r : r + 8])
            lows.append(low)
            highs.append(high)
        out_ref[0, :, cols] = jnp.concatenate(lows, 0).astype(BF16)
        out_ref[1, :, cols] = jnp.concatenate(highs, 0).astype(BF16)


def join_cores(mine, theirs, core):
    rows, depth = mine.shape
    steps = 4
    per = rows // steps
    block = pl.BlockSpec((per, depth), lambda k, w: (k, 0))
    return pl.pallas_call(
        join_kernel,
        grid_spec=pltpu.PrefetchScalarGridSpec(
            num_scalar_prefetch=1,
            grid=(steps,),
            in_specs=[block, block],
            out_specs=pl.BlockSpec((2, per, depth), lambda k, w: (0, k, 0)),
        ),
        out_shape=jax.ShapeDtypeStruct((2, rows, depth), BF16),
        compiler_params=PARAMS,
        name="join_cores",
    )(core, mine, theirs)


def body(step, grads, master, first_moment, second_moment):
    t = step[0]
    power = (t + 1).astype(F32)
    corr = jnp.stack([1.0 - jnp.power(F32(0.9), power), 1.0 - jnp.power(F32(0.95), power)])
    depth = master.shape[-1]
    y, z, core = (lax.axis_index(a).astype(jnp.int32)[None] for a in ZERO)
    at = jnp.concatenate([y, z])
    which = t % 3

    mine, theirs = split_cores(grads[0, 0, 0], core)
    theirs, y, z, at, corr, which = lax.optimization_barrier((theirs, y, z, at, corr, which))
    own, out = add_pair(y, mine, shifted(theirs, "core", 1))
    own, out = add_y(at, own, exchanged(out, "y"))
    new_first, new_second, updated = adam(
        z, corr, own, exchanged(out, "zhi"), master[0], first_moment[0], second_moment[0]
    )
    partner = lax.switch(
        which, [lambda u, d=d: shifted(u, PEER, d) for d in (1, 2, 4)], updated
    )
    averaged = (updated + partner) * 0.5

    whole = averaged.astype(BF16).reshape(8, depth)
    whole = lax.all_gather(whole, "zhi", axis=0, tiled=True)
    whole = lax.all_gather(whole, "y", axis=0, tiled=True)
    whole = join_cores(whole, shifted(whole, "core", 1), core)
    return (averaged[None], new_first[None], new_second[None], whole[None])


def solution(mesh):
    fine = Mesh(mesh.devices.reshape(4, 4, 4, 4, 2), PEER + ZERO)
    shard = P(PEER, None, ZERO, None)
    return jax.shard_map(
        body,
        mesh=fine,
        in_specs=(P(), P(PEER, ZERO, None, None, None, None), shard, shard, shard),
        out_specs=(shard, shard, shard, P(PEER, None, None, None)),
        check_vma=False,
    )
```

```python
import jax
import jax.numpy as jnp
from jax import lax
from jax.experimental import pallas as pl
from jax.experimental.pallas import tpu as pltpu
from jax.sharding import Mesh, PartitionSpec as P

PEER = ("zlo", "x")
ZERO = ("y", "zhi", "core")
F32 = jnp.float32
BF16 = jnp.bfloat16
VMEM = pl.BlockSpec(memory_space=pltpu.VMEM)
SMEM = pl.BlockSpec(memory_space=pltpu.SMEM)
LANES = 512
PARAMS = pltpu.CompilerParams(vmem_limit_bytes=32 * 2**20)


def shifted(block, axis, distance):
    n = lax.axis_size(axis)
    return lax.ppermute(block, axis, [(i, (i + distance) % n) for i in range(n)])


def low_high(a, b):
    row = lax.broadcasted_iota(jnp.int32, a.shape, 0)
    low = jnp.where(row < 4, a, pltpu.roll(b, 4, 0))
    high = jnp.where(row < 4, pltpu.roll(a, 4, 0), b)
    return low, high


def split_kernel(core_ref, grads_ref, mine_ref, theirs_ref):
    first = core_ref[0] == 0
    depth = grads_ref.shape[-1]
    for at in range(0, depth, LANES):
        cols = slice(at, at + LANES)
        a = grads_ref[0, :, cols].astype(F32)
        b = grads_ref[1, :, cols].astype(F32)
        mine, theirs = [], []
        for r in range(0, a.shape[0], 8):
            low, high = low_high(a[r : r + 8], b[r : r + 8])
            mine.append(jnp.where(first, low, high))
            theirs.append(jnp.where(first, high, low))
        mine_ref[0, :, cols] = jnp.concatenate(mine, 0).astype(BF16)
        theirs_ref[0, :, cols] = jnp.concatenate(theirs, 0).astype(BF16)


def split_cores(grads, core):
    layers, rows, depth = grads.shape
    ny = lax.axis_size("y")
    per = rows // ny
    out = jax.ShapeDtypeStruct((ny, per, depth), BF16)
    block = pl.BlockSpec((1, per, depth), lambda k, w: (k, 0, 0))
    return pl.pallas_call(
        split_kernel,
        grid_spec=pltpu.PrefetchScalarGridSpec(
            num_scalar_prefetch=1,
            grid=(ny,),
            in_specs=[pl.BlockSpec((layers, per, depth), lambda k, w: (0, k, 0))],
            out_specs=[block, block],
        ),
        out_shape=(out, out),
        compiler_params=PARAMS,
        name="split_cores",
    )(core, grads)


def scale_of(largest):
    exponent = 14.0 - jnp.floor(jnp.log2(jnp.maximum(largest, 1e-30)))
    return jnp.exp2(exponent), -exponent


def send_scaled(out_ref, sums):
    n, per, _ = out_ref.shape
    depth = sums.shape[-1]
    largest = jnp.zeros((8, LANES), F32)
    for at in range(0, depth, LANES):
        for r in range(0, n * per, 8):
            largest = jnp.maximum(largest, jnp.abs(sums[r : r + 8, at : at + LANES]))
    scale, back = scale_of(jnp.max(largest, axis=(0, 1), keepdims=True))
    for k in range(n):
        for at in range(0, depth, LANES):
            cols = slice(at, at + LANES)
            out_ref[k, :, cols] = sums[k * per : (k + 1) * per, cols] * scale
        out_ref[k, :, depth:] = jnp.broadcast_to(back, (per, out_ref.shape[-1] - depth))


def add_received(total, got_ref, me, cols, depth):
    for k in range(got_ref.shape[0]):
        undo = jnp.exp2(got_ref[k, 0:1, depth : depth + 1])
        total = total + jnp.where(me == k, 0.0, got_ref[k, :, cols] * undo)
    return total


def add_pair_kernel(y_ref, mine_ref, theirs_ref, own_ref, out_ref, sums):
    n, per, depth = mine_ref.shape
    for k in range(n):
        for at in range(0, depth, LANES):
            cols = slice(at, at + LANES)
            sums[k * per : (k + 1) * per, cols] = mine_ref[k, :, cols].astype(F32) + theirs_ref[
                k, :, cols
            ].astype(F32)
    own_ref[...] = sums[pl.ds(pl.multiple_of(y_ref[0] * per, per), per), :]
    send_scaled(out_ref, sums)


def add_pair(y, mine, theirs):
    n, rows, depth = mine.shape
    return pl.pallas_call(
        add_pair_kernel,
        in_specs=[SMEM, VMEM, VMEM],
        out_specs=[VMEM] * 2,
        out_shape=[
            jax.ShapeDtypeStruct((rows, depth), F32),
            jax.ShapeDtypeStruct((n, rows, depth + 128), F32),
        ],
        scratch_shapes=[pltpu.VMEM((n * rows, depth), F32)],
        compiler_params=PARAMS,
        name="add_pair",
    )(y, mine, theirs)


def scaled(block_ref, out_ref):
    depth = block_ref.shape[-1]
    largest = jnp.zeros((8, LANES), F32)
    for at in range(0, depth, LANES):
        largest = jnp.maximum(largest, jnp.abs(block_ref[:, at : at + LANES]))
    scale, back = scale_of(jnp.max(largest, axis=(0, 1), keepdims=True))
    out_ref[:, :depth] = block_ref[...] * scale
    out_ref[:, depth:] = jnp.broadcast_to(back, (8, out_ref.shape[-1] - depth))


def restored(got_ref, depth):
    return got_ref[:, :depth] * jnp.exp2(got_ref[0:1, depth : depth + 1])


def add_y_kernel(at_ref, own_ref, got_ref, keep_ref, near_ref, far_ref, back_ref, sums):
    depth = own_ref.shape[-1]
    n = sums.shape[0] // 8
    for at in range(0, depth, LANES):
        cols = slice(at, at + LANES)
        sums[:, cols] = add_received(own_ref[:, cols], got_ref, at_ref[0], cols, depth)

    def piece(k):
        step = jnp.where(at_ref[2] == 0, k, n - k)
        return pl.ds(pl.multiple_of(((at_ref[1] + step) % n) * 8, 8), 8)

    keep_ref[...] = sums[piece(0), :]
    near_ref[...] = sums[piece(1), :]
    scaled(sums.at[piece(2)], far_ref)
    scaled(sums.at[piece(3)], back_ref)


def add_y(at, own, got):
    rows, depth = own.shape
    kept = jax.ShapeDtypeStruct((8, depth), F32)
    sent = jax.ShapeDtypeStruct((8, depth + 128), F32)
    return pl.pallas_call(
        add_y_kernel,
        in_specs=[SMEM, VMEM, VMEM],
        out_specs=[VMEM] * 4,
        out_shape=[kept, kept, sent, sent],
        scratch_shapes=[pltpu.VMEM((rows, depth), F32)],
        compiler_params=PARAMS,
        name="add_y",
    )(at, own, got)


def add_through_kernel(near_ref, got_ref, out_ref, total):
    total[...] = near_ref[...] + restored(got_ref, near_ref.shape[-1])
    scaled(total, out_ref)


def add_through(near, got):
    return pl.pallas_call(
        add_through_kernel,
        in_specs=[VMEM] * 2,
        out_specs=VMEM,
        out_shape=jax.ShapeDtypeStruct(got.shape, F32),
        scratch_shapes=[pltpu.VMEM(near.shape, F32)],
        compiler_params=PARAMS,
        name="add_through",
    )(near, got)


def turned(block, distance):
    n = lax.axis_size("zhi")
    pairs = []
    for z in range(n):
        pairs.append((2 * z, 2 * ((z + distance) % n)))
        pairs.append((2 * z + 1, 2 * ((z - distance) % n) + 1))
    return lax.ppermute(block.astype(jnp.float16), ("zhi", "core"), pairs).astype(F32)


def exchanged(blocks, axis):
    got = lax.all_to_all(blocks.astype(jnp.float16), axis, 0, 0, tiled=True)
    return got.astype(F32)


def adam_kernel(corr_ref, own_ref, far_ref, back_ref, master_ref, first_ref, second_ref, nf_ref, ns_ref, up_ref):
    depth = own_ref.shape[-1]
    total = own_ref[...] + (restored(far_ref, depth) + restored(back_ref, depth))
    mean_all = total * (1.0 / 32)
    for layer in range(2):
        mean = mean_all[4 * layer : 4 * layer + 4]
        master = master_ref[layer]
        nf = 0.9 * first_ref[layer] + 0.1 * mean
        ns = 0.95 * second_ref[layer] + 0.05 * mean * mean
        nf_ref[layer] = nf
        ns_ref[layer] = ns
        up_ref[layer] = master - 0.05 * (
            nf / corr_ref[0] / (jnp.sqrt(ns / corr_ref[1]) + 1e-08) + 0.1 * master
        )


def adam(corr, own, far, back, master, first, second):
    out = jax.ShapeDtypeStruct(master.shape, F32)
    return pl.pallas_call(
        adam_kernel,
        in_specs=[SMEM] + [VMEM] * 6,
        out_specs=[VMEM] * 3,
        out_shape=[out] * 3,
        compiler_params=PARAMS,
        name="adam",
    )(corr, own, far, back, master, first, second)


def average_kernel(up_ref, partner_ref, out_ref, rounded_ref):
    mean = [(up_ref[i] + partner_ref[i]) * 0.5 for i in range(2)]
    for i in range(2):
        out_ref[i] = mean[i]
    rounded_ref[...] = jnp.concatenate(mean, 0).astype(BF16)


def average(updated, partner):
    layers, rows, depth = updated.shape
    return pl.pallas_call(
        average_kernel,
        in_specs=[VMEM] * 2,
        out_specs=[VMEM] * 2,
        out_shape=[
            jax.ShapeDtypeStruct(updated.shape, F32),
            jax.ShapeDtypeStruct((layers * rows, depth), BF16),
        ],
        compiler_params=PARAMS,
        name="average",
    )(updated, partner)


def join_kernel(core_ref, mine_ref, theirs_ref, out_ref):
    first = core_ref[0] == 0
    depth = mine_ref.shape[-1]
    for at in range(0, depth, LANES):
        cols = slice(at, at + LANES)
        mine = mine_ref[:, cols].astype(F32)
        theirs = theirs_ref[:, cols].astype(F32)
        a = jnp.where(first, mine, theirs)
        b = jnp.where(first, theirs, mine)
        lows, highs = [], []
        for r in range(0, a.shape[0], 8):
            low, high = low_high(a[r : r + 8], b[r : r + 8])
            lows.append(low)
            highs.append(high)
        out_ref[0, :, cols] = jnp.concatenate(lows, 0).astype(BF16)
        out_ref[1, :, cols] = jnp.concatenate(highs, 0).astype(BF16)


def join_cores(mine, theirs, core):
    rows, depth = mine.shape
    steps = 4
    per = rows // steps
    block = pl.BlockSpec((per, depth), lambda k, w: (k, 0))
    return pl.pallas_call(
        join_kernel,
        grid_spec=pltpu.PrefetchScalarGridSpec(
            num_scalar_prefetch=1,
            grid=(steps,),
            in_specs=[block, block],
            out_specs=pl.BlockSpec((2, per, depth), lambda k, w: (0, k, 0)),
        ),
        out_shape=jax.ShapeDtypeStruct((2, rows, depth), BF16),
        compiler_params=PARAMS,
        name="join_cores",
    )(core, mine, theirs)


def body(step, grads, master, first_moment, second_moment):
    t = step[0]
    power = (t + 1).astype(F32)
    corr = jnp.stack([1.0 - jnp.power(F32(0.9), power), 1.0 - jnp.power(F32(0.95), power)])
    y, z, core = (lax.axis_index(a).astype(jnp.int32)[None] for a in ZERO)
    at = jnp.concatenate([y, z, core])

    mine, theirs = split_cores(grads[0, 0, 0], core)
    theirs = shifted(theirs, "core", 1)
    theirs, y, at, corr = lax.optimization_barrier((theirs, y, at, corr))
    own, out = add_pair(y, mine, theirs)
    own, near, far, back = add_y(at, own, exchanged(out, "y"))
    far = turned(far, 1)
    back = turned(back, -1)
    far = turned(add_through(near, far), 1)
    new_first, new_second, updated = adam(
        corr, own, back, far, master[0], first_moment[0], second_moment[0]
    )
    partner = lax.switch(
        t % 3, [lambda u, d=d: shifted(u, PEER, d) for d in (1, 2, 4)], updated
    )
    averaged, whole = average(updated, partner)
    whole = lax.all_gather(whole, "zhi", axis=0, tiled=True)
    whole = lax.all_gather(whole, "y", axis=0, tiled=True)
    whole = join_cores(whole, shifted(whole, "core", 1), core)
    return (averaged[None], new_first[None], new_second[None], whole[None])


def solution(mesh):
    fine = Mesh(mesh.devices.reshape(4, 4, 4, 4, 2), PEER + ZERO)
    shard = P(PEER, None, ZERO, None)
    return jax.shard_map(
        body,
        mesh=fine,
        in_specs=(P(), P(PEER, ZERO, None, None, None, None), shard, shard, shard),
        out_specs=(shard, shard, shard, P(PEER, None, None, None)),
        check_vma=False,
    )
```

```python
import jax
import jax.numpy as jnp
from jax import lax
from jax.experimental import pallas as pl
from jax.experimental.pallas import tpu as pltpu
from jax.sharding import Mesh, PartitionSpec as P

PEER = ("zlo", "x")
ZERO = ("y", "zhi", "core")
F32 = jnp.float32
BF16 = jnp.bfloat16
VMEM = pl.BlockSpec(memory_space=pltpu.VMEM)
SMEM = pl.BlockSpec(memory_space=pltpu.SMEM)
LANES = 512
PARAMS = pltpu.CompilerParams(vmem_limit_bytes=32 * 2**20)


def shifted(block, axis, distance):
    n = lax.axis_size(axis)
    return lax.ppermute(block, axis, [(i, (i + distance) % n) for i in range(n)])


def low_high(a, b):
    row = lax.broadcasted_iota(jnp.int32, a.shape, 0)
    low = jnp.where(row < 4, a, pltpu.roll(b, 4, 0))
    high = jnp.where(row < 4, pltpu.roll(a, 4, 0), b)
    return low, high


def split_kernel(core_ref, grads_ref, mine_ref, theirs_ref, held, sems):
    first = core_ref[0] == 0
    n, _, per, depth = held.shape
    copies = [
        pltpu.make_async_copy(
            grads_ref.at[:, k * per : (k + 1) * per, :], held.at[k], sems.at[k]
        )
        for k in range(n)
    ]
    for copy in copies:
        copy.start()
    for k, copy in enumerate(copies):
        copy.wait()
        for at in range(0, depth, LANES):
            cols = slice(at, at + LANES)
            a = held[k, 0, :, cols].astype(F32)
            b = held[k, 1, :, cols].astype(F32)
            mine, theirs = [], []
            for r in range(0, per, 8):
                low, high = low_high(a[r : r + 8], b[r : r + 8])
                mine.append(jnp.where(first, low, high))
                theirs.append(jnp.where(first, high, low))
            mine_ref[k, :, cols] = jnp.concatenate(mine, 0).astype(BF16)
            theirs_ref[k, :, cols] = jnp.concatenate(theirs, 0).astype(BF16)


def split_cores(grads, core):
    layers, rows, depth = grads.shape
    ny = lax.axis_size("y")
    per = rows // ny
    out = jax.ShapeDtypeStruct((ny, per, depth), BF16)
    return pl.pallas_call(
        split_kernel,
        in_specs=[SMEM, pl.BlockSpec(memory_space=pltpu.HBM)],
        out_specs=[VMEM] * 2,
        out_shape=(out, out),
        scratch_shapes=[
            pltpu.VMEM((ny, layers, per, depth), BF16),
            pltpu.SemaphoreType.DMA((ny,)),
        ],
        compiler_params=pltpu.CompilerParams(vmem_limit_bytes=52 * 2**20),
        name="split_cores",
    )(core, grads)


def scale_of(largest):
    exponent = 14.0 - jnp.floor(jnp.log2(jnp.maximum(largest, 1e-30)))
    return jnp.exp2(exponent), -exponent


def send_scaled(out_ref, sums):
    n, per, _ = out_ref.shape
    depth = sums.shape[-1]
    largest = jnp.zeros((8, LANES), F32)
    for at in range(0, depth, LANES):
        for r in range(0, n * per, 8):
            largest = jnp.maximum(largest, jnp.abs(sums[r : r + 8, at : at + LANES]))
    scale, back = scale_of(jnp.max(largest, axis=(0, 1), keepdims=True))
    for k in range(n):
        for at in range(0, depth, LANES):
            cols = slice(at, at + LANES)
            out_ref[k, :, cols] = sums[k * per : (k + 1) * per, cols] * scale
        out_ref[k, :, depth:] = jnp.broadcast_to(back, (per, out_ref.shape[-1] - depth))


def add_received(total, got_ref, me, cols, depth):
    for k in range(got_ref.shape[0]):
        undo = jnp.exp2(got_ref[k, 0:1, depth : depth + 1])
        total = total + jnp.where(me == k, 0.0, got_ref[k, :, cols] * undo)
    return total


def add_pair_kernel(y_ref, mine_ref, theirs_ref, own_ref, out_ref, sums):
    n, per, depth = mine_ref.shape
    for k in range(n):
        for at in range(0, depth, LANES):
            cols = slice(at, at + LANES)
            sums[k * per : (k + 1) * per, cols] = mine_ref[k, :, cols].astype(F32) + theirs_ref[
                k, :, cols
            ].astype(F32)
    own_ref[...] = sums[pl.ds(pl.multiple_of(y_ref[0] * per, per), per), :]
    send_scaled(out_ref, sums)


def add_pair(y, mine, theirs):
    n, rows, depth = mine.shape
    return pl.pallas_call(
        add_pair_kernel,
        in_specs=[SMEM, VMEM, VMEM],
        out_specs=[VMEM] * 2,
        out_shape=[
            jax.ShapeDtypeStruct((rows, depth), F32),
            jax.ShapeDtypeStruct((n, rows, depth + 128), F32),
        ],
        scratch_shapes=[pltpu.VMEM((n * rows, depth), F32)],
        compiler_params=PARAMS,
        name="add_pair",
    )(y, mine, theirs)


def scaled(block_ref, out_ref):
    depth = block_ref.shape[-1]
    largest = jnp.zeros((8, LANES), F32)
    for at in range(0, depth, LANES):
        largest = jnp.maximum(largest, jnp.abs(block_ref[:, at : at + LANES]))
    scale, back = scale_of(jnp.max(largest, axis=(0, 1), keepdims=True))
    out_ref[:, :depth] = block_ref[...] * scale
    out_ref[:, depth:] = jnp.broadcast_to(back, (8, out_ref.shape[-1] - depth))


def restored(got_ref, depth):
    return got_ref[:, :depth] * jnp.exp2(got_ref[0:1, depth : depth + 1])


def add_y_kernel(at_ref, own_ref, got_ref, keep_ref, near_ref, far_ref, back_ref, sums):
    depth = own_ref.shape[-1]
    n = sums.shape[0] // 8
    for at in range(0, depth, LANES):
        cols = slice(at, at + LANES)
        sums[:, cols] = add_received(own_ref[:, cols], got_ref, at_ref[0], cols, depth)

    def piece(k):
        step = jnp.where(at_ref[2] == 0, k, n - k)
        return pl.ds(pl.multiple_of(((at_ref[1] + step) % n) * 8, 8), 8)

    keep_ref[...] = sums[piece(0), :]
    near_ref[...] = sums[piece(1), :]
    scaled(sums.at[piece(2)], far_ref)
    scaled(sums.at[piece(3)], back_ref)


def add_y(at, own, got):
    rows, depth = own.shape
    kept = jax.ShapeDtypeStruct((8, depth), F32)
    sent = jax.ShapeDtypeStruct((8, depth + 128), F32)
    return pl.pallas_call(
        add_y_kernel,
        in_specs=[SMEM, VMEM, VMEM],
        out_specs=[VMEM] * 4,
        out_shape=[kept, kept, sent, sent],
        scratch_shapes=[pltpu.VMEM((rows, depth), F32)],
        compiler_params=PARAMS,
        name="add_y",
    )(at, own, got)


def add_through_kernel(near_ref, got_ref, out_ref, total):
    total[...] = near_ref[...] + restored(got_ref, near_ref.shape[-1])
    scaled(total, out_ref)


def add_through(near, got):
    return pl.pallas_call(
        add_through_kernel,
        in_specs=[VMEM] * 2,
        out_specs=VMEM,
        out_shape=jax.ShapeDtypeStruct(got.shape, F32),
        scratch_shapes=[pltpu.VMEM(near.shape, F32)],
        compiler_params=PARAMS,
        name="add_through",
    )(near, got)


def turned(block, distance):
    n = lax.axis_size("zhi")
    pairs = []
    for z in range(n):
        pairs.append((2 * z, 2 * ((z + distance) % n)))
        pairs.append((2 * z + 1, 2 * ((z - distance) % n) + 1))
    return lax.ppermute(block.astype(jnp.float16), ("zhi", "core"), pairs).astype(F32)


def exchanged(blocks, axis):
    got = lax.all_to_all(blocks.astype(jnp.float16), axis, 0, 0, tiled=True)
    return got.astype(F32)


def moments(mean, first, second):
    return 0.9 * first + 0.1 * mean, 0.95 * second + 0.05 * mean * mean


def adam_kernel(corr_ref, own_ref, far_ref, back_ref, master_ref, first_ref, second_ref, mean_ref, up_ref):
    depth = own_ref.shape[-1]
    total = own_ref[...] + (restored(far_ref, depth) + restored(back_ref, depth))
    mean_all = total * (1.0 / 32)
    mean_ref[...] = mean_all
    for layer in range(2):
        mean = mean_all[4 * layer : 4 * layer + 4]
        master = master_ref[layer]
        nf, ns = moments(mean, first_ref[layer], second_ref[layer])
        up_ref[layer] = master - 0.05 * (
            nf / corr_ref[0] / (jnp.sqrt(ns / corr_ref[1]) + 1e-08) + 0.1 * master
        )


def adam(corr, own, far, back, master, first, second):
    return pl.pallas_call(
        adam_kernel,
        in_specs=[SMEM] + [VMEM] * 6,
        out_specs=[VMEM] * 2,
        out_shape=[
            jax.ShapeDtypeStruct(own.shape, F32),
            jax.ShapeDtypeStruct(master.shape, F32),
        ],
        compiler_params=PARAMS,
        name="adam",
    )(corr, own, far, back, master, first, second)


def average_kernel(up_ref, partner_ref, rounded_ref):
    mean = [(up_ref[i] + partner_ref[i]) * 0.5 for i in range(2)]
    rounded_ref[...] = jnp.concatenate(mean, 0).astype(BF16)


def average(updated, partner):
    layers, rows, depth = updated.shape
    return pl.pallas_call(
        average_kernel,
        in_specs=[VMEM] * 2,
        out_specs=VMEM,
        out_shape=jax.ShapeDtypeStruct((layers * rows, depth), BF16),
        compiler_params=PARAMS,
        name="average",
    )(updated, partner)


def finish_kernel(mean_ref, first_ref, second_ref, up_ref, partner_ref, out_ref, nf_ref, ns_ref):
    for layer in range(2):
        mean = mean_ref[4 * layer : 4 * layer + 4, :]
        nf, ns = moments(mean, first_ref[layer], second_ref[layer])
        nf_ref[layer] = nf
        ns_ref[layer] = ns
        out_ref[layer] = (up_ref[layer] + partner_ref[layer]) * 0.5


def finish(mean, first, second, updated, partner):
    return pl.pallas_call(
        finish_kernel,
        in_specs=[VMEM] * 5,
        out_specs=[VMEM] * 3,
        out_shape=[jax.ShapeDtypeStruct(first.shape, F32)] * 3,
        compiler_params=PARAMS,
        name="finish",
    )(mean, first, second, updated, partner)


def join_kernel(core_ref, mine_ref, theirs_ref, out_ref, held, sems):
    first = core_ref[0] == 0
    n, _, per, depth = held.shape
    copies = []
    for k in range(n):
        rows = slice(k * per, (k + 1) * per)
        for at in range(0, depth, LANES):
            cols = slice(at, at + LANES)
            mine = mine_ref[rows, cols].astype(F32)
            theirs = theirs_ref[rows, cols].astype(F32)
            a = jnp.where(first, mine, theirs)
            b = jnp.where(first, theirs, mine)
            lows, highs = [], []
            for r in range(0, per, 8):
                low, high = low_high(a[r : r + 8], b[r : r + 8])
                lows.append(low)
                highs.append(high)
            held[k, 0, :, cols] = jnp.concatenate(lows, 0).astype(BF16)
            held[k, 1, :, cols] = jnp.concatenate(highs, 0).astype(BF16)
        copies.append(pltpu.make_async_copy(held.at[k], out_ref.at[:, rows, :], sems.at[k]))
        copies[k].start()
    for copy in copies:
        copy.wait()


def join_cores(mine, theirs, core):
    rows, depth = mine.shape
    steps = 4
    return pl.pallas_call(
        join_kernel,
        in_specs=[SMEM, VMEM, VMEM],
        out_specs=pl.BlockSpec(memory_space=pltpu.HBM),
        out_shape=jax.ShapeDtypeStruct((2, rows, depth), BF16),
        scratch_shapes=[
            pltpu.VMEM((steps, 2, rows // steps, depth), BF16),
            pltpu.SemaphoreType.DMA((steps,)),
        ],
        compiler_params=PARAMS,
        name="join_cores",
    )(core, mine, theirs)


def body(step, grads, master, first_moment, second_moment):
    t = step[0]
    power = (t + 1).astype(F32)
    corr = jnp.stack([1.0 - jnp.power(F32(0.9), power), 1.0 - jnp.power(F32(0.95), power)])
    y, z, core = (lax.axis_index(a).astype(jnp.int32)[None] for a in ZERO)
    at = jnp.concatenate([y, z, core])

    mine, theirs = split_cores(grads[0, 0, 0], core)
    theirs = shifted(theirs, "core", 1)
    theirs, y, at, corr = lax.optimization_barrier((theirs, y, at, corr))
    own, out = add_pair(y, mine, theirs)
    own, near, far, back = add_y(at, own, exchanged(out, "y"))
    far = turned(far, 1)
    back = turned(back, -1)
    far = turned(add_through(near, far), 1)
    mean, updated = adam(
        corr, own, back, far, master[0], first_moment[0], second_moment[0]
    )
    partner = lax.switch(
        t % 3, [lambda u, d=d: shifted(u, PEER, d) for d in (1, 2, 4)], updated
    )
    whole = average(updated, partner)
    whole = lax.all_gather(whole, "zhi", axis=0, tiled=True)
    whole = lax.all_gather(whole, "y", axis=0, tiled=True)
    whole, mean, updated, partner = lax.optimization_barrier((whole, mean, updated, partner))
    other = shifted(whole, "core", 1)
    averaged, new_first, new_second = finish(
        mean, first_moment[0], second_moment[0], updated, partner
    )
    whole = join_cores(whole, other, core)
    return (averaged[None], new_first[None], new_second[None], whole[None])


def solution(mesh):
    fine = Mesh(mesh.devices.reshape(4, 4, 4, 4, 2), PEER + ZERO)
    shard = P(PEER, None, ZERO, None)
    return jax.shard_map(
        body,
        mesh=fine,
        in_specs=(P(), P(PEER, ZERO, None, None, None, None), shard, shard, shard),
        out_specs=(shard, shard, shard, P(PEER, None, None, None)),
        check_vma=False,
    )
```

```python
import jax
import jax.numpy as jnp
from jax import lax
from jax.experimental import pallas as pl
from jax.experimental.pallas import tpu as pltpu
from jax.sharding import Mesh, PartitionSpec as P

PEER = ("zlo", "x")
ZERO = ("y", "zhi", "core")
F32 = jnp.float32
BF16 = jnp.bfloat16
VMEM = pl.BlockSpec(memory_space=pltpu.VMEM)
SMEM = pl.BlockSpec(memory_space=pltpu.SMEM)
LANES = 512
PARAMS = pltpu.CompilerParams(vmem_limit_bytes=32 * 2**20)


def shifted(block, axis, distance):
    n = lax.axis_size(axis)
    return lax.ppermute(block, axis, [(i, (i + distance) % n) for i in range(n)])


def low_high(a, b):
    row = lax.broadcasted_iota(jnp.int32, a.shape, 0)
    low = jnp.where(row < 4, a, pltpu.roll(b, 4, 0))
    high = jnp.where(row < 4, pltpu.roll(a, 4, 0), b)
    return low, high


def split_kernel(core_ref, grads_ref, mine_ref, theirs_ref, held, sems):
    first = core_ref[0] == 0
    n, _, per, depth = held.shape
    copies = [
        pltpu.make_async_copy(
            grads_ref.at[:, k * per : (k + 1) * per, :], held.at[k], sems.at[k]
        )
        for k in range(n)
    ]
    for copy in copies:
        copy.start()
    for k, copy in enumerate(copies):
        copy.wait()
        for at in range(0, depth, LANES):
            cols = slice(at, at + LANES)
            a = held[k, 0, :, cols].astype(F32)
            b = held[k, 1, :, cols].astype(F32)
            mine, theirs = [], []
            for r in range(0, per, 8):
                low, high = low_high(a[r : r + 8], b[r : r + 8])
                mine.append(jnp.where(first, low, high))
                theirs.append(jnp.where(first, high, low))
            mine_ref[k, :, cols] = jnp.concatenate(mine, 0).astype(BF16)
            theirs_ref[k, :, cols] = jnp.concatenate(theirs, 0).astype(BF16)


def split_cores(grads, core):
    layers, rows, depth = grads.shape
    ny = lax.axis_size("y")
    per = rows // ny
    out = jax.ShapeDtypeStruct((ny, per, depth), BF16)
    return pl.pallas_call(
        split_kernel,
        in_specs=[SMEM, pl.BlockSpec(memory_space=pltpu.HBM)],
        out_specs=[VMEM] * 2,
        out_shape=(out, out),
        scratch_shapes=[
            pltpu.VMEM((ny, layers, per, depth), BF16),
            pltpu.SemaphoreType.DMA((ny,)),
        ],
        compiler_params=pltpu.CompilerParams(vmem_limit_bytes=52 * 2**20),
        name="split_cores",
    )(core, grads)


def scale_of(largest):
    exponent = 14.0 - jnp.floor(jnp.log2(jnp.maximum(largest, 1e-30)))
    return jnp.exp2(exponent), -exponent


def add_pair_kernel(at_ref, mine_ref, theirs_ref, own_ref, near_ref, far_ref, back_ref, sums):
    n, per, depth = mine_ref.shape
    largest = jnp.zeros((8, LANES), F32)
    for k in range(n):
        for at in range(0, depth, LANES):
            cols = slice(at, at + LANES)
            total = mine_ref[k, :, cols].astype(F32) + theirs_ref[k, :, cols].astype(F32)
            sums[k * per : (k + 1) * per, cols] = total
            for r in range(0, per, 8):
                largest = jnp.maximum(largest, jnp.abs(total[r : r + 8]))
    scale, back = scale_of(jnp.max(largest, axis=(0, 1), keepdims=True))

    def piece(k):
        step = jnp.where(at_ref[2] == 0, k, n - k)
        return pl.ds(pl.multiple_of(((at_ref[0] + step) % n) * per, per), per)

    own_ref[...] = sums[piece(0), :]
    for k, out_ref in ((1, near_ref), (2, far_ref), (3, back_ref)):
        rows = piece(k)
        for at in range(0, depth, LANES):
            cols = slice(at, at + LANES)
            out_ref[:, cols] = sums[rows, cols] * scale
        out_ref[:, depth:] = jnp.broadcast_to(back, (per, out_ref.shape[-1] - depth))


def add_pair(at, mine, theirs):
    n, rows, depth = mine.shape
    return pl.pallas_call(
        add_pair_kernel,
        in_specs=[SMEM, VMEM, VMEM],
        out_specs=[VMEM] * 4,
        out_shape=[jax.ShapeDtypeStruct((rows, depth), F32)]
        + [jax.ShapeDtypeStruct((rows, depth + 128), F32)] * 3,
        scratch_shapes=[pltpu.VMEM((n * rows, depth), F32)],
        compiler_params=PARAMS,
        name="add_pair",
    )(at, mine, theirs)


def scaled(block_ref, out_ref):
    depth = block_ref.shape[-1]
    largest = jnp.zeros((8, LANES), F32)
    for at in range(0, depth, LANES):
        largest = jnp.maximum(largest, jnp.abs(block_ref[:, at : at + LANES]))
    scale, back = scale_of(jnp.max(largest, axis=(0, 1), keepdims=True))
    out_ref[:, :depth] = block_ref[...] * scale
    out_ref[:, depth:] = jnp.broadcast_to(back, (8, out_ref.shape[-1] - depth))


def restored(got_ref, depth):
    return got_ref[:, :depth] * jnp.exp2(got_ref[0:1, depth : depth + 1])


def add_y_kernel(at_ref, own_ref, a_ref, b_ref, c_ref, keep_ref, near_ref, far_ref, back_ref, sums):
    depth = own_ref.shape[-1]
    n = sums.shape[0] // 8
    for at in range(0, depth, LANES):
        cols = slice(at, at + LANES)
        total = own_ref[:, cols]
        for got_ref in (a_ref, b_ref, c_ref):
            total = total + got_ref[:, cols] * jnp.exp2(got_ref[0:1, depth : depth + 1])
        sums[:, cols] = total

    def piece(k):
        step = jnp.where(at_ref[2] == 0, k, n - k)
        return pl.ds(pl.multiple_of(((at_ref[1] + step) % n) * 8, 8), 8)

    keep_ref[...] = sums[piece(0), :]
    near_ref[...] = sums[piece(1), :]
    scaled(sums.at[piece(2)], far_ref)
    scaled(sums.at[piece(3)], back_ref)


def add_y(at, own, parts):
    rows, depth = own.shape
    kept = jax.ShapeDtypeStruct((8, depth), F32)
    sent = jax.ShapeDtypeStruct((8, depth + 128), F32)
    return pl.pallas_call(
        add_y_kernel,
        in_specs=[SMEM] + [VMEM] * 4,
        out_specs=[VMEM] * 4,
        out_shape=[kept, kept, sent, sent],
        scratch_shapes=[pltpu.VMEM((rows, depth), F32)],
        compiler_params=PARAMS,
        name="add_y",
    )(at, own, *parts)


def add_through_kernel(near_ref, got_ref, out_ref, total):
    total[...] = near_ref[...] + restored(got_ref, near_ref.shape[-1])
    scaled(total, out_ref)


def add_through(near, got):
    return pl.pallas_call(
        add_through_kernel,
        in_specs=[VMEM] * 2,
        out_specs=VMEM,
        out_shape=jax.ShapeDtypeStruct(got.shape, F32),
        scratch_shapes=[pltpu.VMEM(near.shape, F32)],
        compiler_params=PARAMS,
        name="add_through",
    )(near, got)


def turned(block, axis, distance):
    n = lax.axis_size(axis)
    pairs = []
    for i in range(n):
        pairs.append((2 * i, 2 * ((i + distance) % n)))
        pairs.append((2 * i + 1, 2 * ((i - distance) % n) + 1))
    return lax.ppermute(block.astype(jnp.float16), (axis, "core"), pairs).astype(F32)


def moments(mean, first, second):
    return 0.9 * first + 0.1 * mean, 0.95 * second + 0.05 * mean * mean


def adam_kernel(corr_ref, own_ref, far_ref, back_ref, master_ref, first_ref, second_ref, mean_ref, up_ref):
    depth = own_ref.shape[-1]
    total = own_ref[...] + (restored(far_ref, depth) + restored(back_ref, depth))
    mean_all = total * (1.0 / 32)
    mean_ref[...] = mean_all
    for layer in range(2):
        mean = mean_all[4 * layer : 4 * layer + 4]
        master = master_ref[layer]
        nf, ns = moments(mean, first_ref[layer], second_ref[layer])
        up_ref[layer] = master - 0.05 * (
            nf / corr_ref[0] / (jnp.sqrt(ns / corr_ref[1]) + 1e-08) + 0.1 * master
        )


def adam(corr, own, far, back, master, first, second):
    return pl.pallas_call(
        adam_kernel,
        in_specs=[SMEM] + [VMEM] * 6,
        out_specs=[VMEM] * 2,
        out_shape=[
            jax.ShapeDtypeStruct(own.shape, F32),
            jax.ShapeDtypeStruct(master.shape, F32),
        ],
        compiler_params=PARAMS,
        name="adam",
    )(corr, own, far, back, master, first, second)


def average_kernel(up_ref, partner_ref, rounded_ref):
    mean = [(up_ref[i] + partner_ref[i]) * 0.5 for i in range(2)]
    rounded_ref[...] = jnp.concatenate(mean, 0).astype(BF16)


def average(updated, partner):
    layers, rows, depth = updated.shape
    return pl.pallas_call(
        average_kernel,
        in_specs=[VMEM] * 2,
        out_specs=VMEM,
        out_shape=jax.ShapeDtypeStruct((layers * rows, depth), BF16),
        compiler_params=PARAMS,
        name="average",
    )(updated, partner)


def finish_kernel(mean_ref, first_ref, second_ref, up_ref, partner_ref, out_ref, nf_ref, ns_ref):
    for layer in range(2):
        mean = mean_ref[4 * layer : 4 * layer + 4, :]
        nf, ns = moments(mean, first_ref[layer], second_ref[layer])
        nf_ref[layer] = nf
        ns_ref[layer] = ns
        out_ref[layer] = (up_ref[layer] + partner_ref[layer]) * 0.5


def finish(mean, first, second, updated, partner):
    return pl.pallas_call(
        finish_kernel,
        in_specs=[VMEM] * 5,
        out_specs=[VMEM] * 3,
        out_shape=[jax.ShapeDtypeStruct(first.shape, F32)] * 3,
        compiler_params=PARAMS,
        name="finish",
    )(mean, first, second, updated, partner)


def join_kernel(core_ref, mine_ref, theirs_ref, out_ref, held, sems):
    first = core_ref[0] == 0
    n, _, per, depth = held.shape
    copies = []
    for k in range(n):
        rows = slice(k * per, (k + 1) * per)
        for at in range(0, depth, LANES):
            cols = slice(at, at + LANES)
            mine = mine_ref[rows, cols].astype(F32)
            theirs = theirs_ref[rows, cols].astype(F32)
            a = jnp.where(first, mine, theirs)
            b = jnp.where(first, theirs, mine)
            lows, highs = [], []
            for r in range(0, per, 8):
                low, high = low_high(a[r : r + 8], b[r : r + 8])
                lows.append(low)
                highs.append(high)
            held[k, 0, :, cols] = jnp.concatenate(lows, 0).astype(BF16)
            held[k, 1, :, cols] = jnp.concatenate(highs, 0).astype(BF16)
        copies.append(pltpu.make_async_copy(held.at[k], out_ref.at[:, rows, :], sems.at[k]))
        copies[k].start()
    for copy in copies:
        copy.wait()


def join_cores(mine, theirs, core):
    rows, depth = mine.shape
    steps = 4
    return pl.pallas_call(
        join_kernel,
        in_specs=[SMEM, VMEM, VMEM],
        out_specs=pl.BlockSpec(memory_space=pltpu.HBM),
        out_shape=jax.ShapeDtypeStruct((2, rows, depth), BF16),
        scratch_shapes=[
            pltpu.VMEM((steps, 2, rows // steps, depth), BF16),
            pltpu.SemaphoreType.DMA((steps,)),
        ],
        compiler_params=PARAMS,
        name="join_cores",
    )(core, mine, theirs)


def body(step, grads, master, first_moment, second_moment):
    t = step[0]
    power = (t + 1).astype(F32)
    corr = jnp.stack([1.0 - jnp.power(F32(0.9), power), 1.0 - jnp.power(F32(0.95), power)])
    y, z, core = (lax.axis_index(a).astype(jnp.int32)[None] for a in ZERO)
    at = jnp.concatenate([y, z, core])

    mine, theirs = split_cores(grads[0, 0, 0], core)
    theirs = shifted(theirs, "core", 1)
    theirs, at, corr = lax.optimization_barrier((theirs, at, corr))
    own, near, far, back = add_pair(at, mine, theirs)
    parts = [turned(near, "y", 1), turned(back, "y", -1), turned(far, "y", 2)]
    own, near, far, back = add_y(at, own, parts)
    far = turned(far, "zhi", 1)
    back = turned(back, "zhi", -1)
    far = turned(add_through(near, far), "zhi", 1)
    mean, updated = adam(
        corr, own, back, far, master[0], first_moment[0], second_moment[0]
    )
    partner = lax.switch(
        t % 3, [lambda u, d=d: shifted(u, PEER, d) for d in (1, 2, 4)], updated
    )
    whole = average(updated, partner)
    whole = lax.all_gather(whole, "zhi", axis=0, tiled=True)
    whole = lax.all_gather(whole, "y", axis=0, tiled=True)
    whole, mean, updated, partner = lax.optimization_barrier((whole, mean, updated, partner))
    other = shifted(whole, "core", 1)
    averaged, new_first, new_second = finish(
        mean, first_moment[0], second_moment[0], updated, partner
    )
    whole = join_cores(whole, other, core)
    return (averaged[None], new_first[None], new_second[None], whole[None])


def solution(mesh):
    fine = Mesh(mesh.devices.reshape(4, 4, 4, 4, 2), PEER + ZERO)
    shard = P(PEER, None, ZERO, None)
    return jax.shard_map(
        body,
        mesh=fine,
        in_specs=(P(), P(PEER, ZERO, None, None, None, None), shard, shard, shard),
        out_specs=(shard, shard, shard, P(PEER, None, None, None)),
        check_vma=False,
    )
```

```python
import functools

import jax
import jax.numpy as jnp
from jax import lax
from jax.experimental import pallas as pl
from jax.experimental.pallas import tpu as pltpu
from jax.sharding import Mesh, PartitionSpec as P

PEER = ("zlo", "x")
ZERO = ("y", "zhi", "core")
F32 = jnp.float32
BF16 = jnp.bfloat16
VMEM = pl.BlockSpec(memory_space=pltpu.VMEM)
SMEM = pl.BlockSpec(memory_space=pltpu.SMEM)
LANES = 512
PARAMS = pltpu.CompilerParams(vmem_limit_bytes=32 * 2**20)


def shifted(block, axis, distance):
    n = lax.axis_size(axis)
    return lax.ppermute(block, axis, [(i, (i + distance) % n) for i in range(n)])


def low_high(a, b):
    row = lax.broadcasted_iota(jnp.int32, a.shape, 0)
    low = jnp.where(row < 4, a, pltpu.roll(b, 4, 0))
    high = jnp.where(row < 4, pltpu.roll(a, 4, 0), b)
    return low, high


def split_kernel(core_ref, grads_ref, mine_ref, theirs_ref, held, sems):
    first = core_ref[0] == 0
    n, _, per, depth = held.shape
    copies = [
        pltpu.make_async_copy(
            grads_ref.at[:, k * per : (k + 1) * per, :], held.at[k], sems.at[k]
        )
        for k in range(n)
    ]
    for copy in copies:
        copy.start()
    for k, copy in enumerate(copies):
        copy.wait()
        for at in range(0, depth, LANES):
            cols = slice(at, at + LANES)
            a = held[k, 0, :, cols].astype(F32)
            b = held[k, 1, :, cols].astype(F32)
            mine, theirs = [], []
            for r in range(0, per, 8):
                low, high = low_high(a[r : r + 8], b[r : r + 8])
                mine.append(jnp.where(first, low, high))
                theirs.append(jnp.where(first, high, low))
            mine_ref[k, :, cols] = jnp.concatenate(mine, 0).astype(BF16)
            theirs_ref[k, :, cols] = jnp.concatenate(theirs, 0).astype(BF16)


def split_cores(grads, core):
    layers, rows, depth = grads.shape
    ny = lax.axis_size("y")
    per = rows // ny
    out = jax.ShapeDtypeStruct((ny, per, depth), BF16)
    return pl.pallas_call(
        split_kernel,
        in_specs=[SMEM, pl.BlockSpec(memory_space=pltpu.HBM)],
        out_specs=[VMEM] * 2,
        out_shape=(out, out),
        scratch_shapes=[
            pltpu.VMEM((ny, layers, per, depth), BF16),
            pltpu.SemaphoreType.DMA((ny,)),
        ],
        compiler_params=pltpu.CompilerParams(vmem_limit_bytes=52 * 2**20),
        name="split_cores",
    )(core, grads)


def scale_of(largest):
    exponent = 14.0 - jnp.floor(jnp.log2(jnp.maximum(largest, 1e-30)))
    return jnp.exp2(exponent), -exponent


def add_pair_kernel(step, at_ref, mine_ref, theirs_ref, out_ref, sums):
    n, per, depth = mine_ref.shape
    ahead = step if step == 2 else jnp.where(at_ref[2] == 0, step, n - step)
    y = (at_ref[0] + ahead) % n
    largest = jnp.zeros((8, LANES), F32)
    for at in range(0, depth, LANES):
        cols = slice(at, at + LANES)
        total = mine_ref[y, :, cols].astype(F32) + theirs_ref[y, :, cols].astype(F32)
        sums[:, cols] = total
        for r in range(0, per, 8):
            largest = jnp.maximum(largest, jnp.abs(total[r : r + 8]))
    scale, back = scale_of(jnp.max(largest, axis=(0, 1), keepdims=True))
    for at in range(0, depth, LANES):
        cols = slice(at, at + LANES)
        out_ref[:, cols] = sums[:, cols] * scale
    out_ref[:, depth:] = jnp.broadcast_to(back, (per, out_ref.shape[-1] - depth))


def add_pair(step, at, mine, theirs):
    _, rows, depth = mine.shape
    return pl.pallas_call(
        functools.partial(add_pair_kernel, step),
        in_specs=[SMEM, VMEM, VMEM],
        out_specs=VMEM,
        out_shape=jax.ShapeDtypeStruct((rows, depth + 128), F32),
        scratch_shapes=[pltpu.VMEM((rows, depth), F32)],
        compiler_params=PARAMS,
        name=f"add_pair_{step}",
    )(at, mine, theirs)


def scaled(block_ref, out_ref):
    depth = block_ref.shape[-1]
    largest = jnp.zeros((8, LANES), F32)
    for at in range(0, depth, LANES):
        largest = jnp.maximum(largest, jnp.abs(block_ref[:, at : at + LANES]))
    scale, back = scale_of(jnp.max(largest, axis=(0, 1), keepdims=True))
    out_ref[:, :depth] = block_ref[...] * scale
    out_ref[:, depth:] = jnp.broadcast_to(back, (8, out_ref.shape[-1] - depth))


def restored(got_ref, depth):
    return got_ref[:, :depth] * jnp.exp2(got_ref[0:1, depth : depth + 1])


def add_y_kernel(at_ref, mine_ref, theirs_ref, a_ref, b_ref, c_ref, keep_ref, near_ref, far_ref, back_ref, sums):
    depth = mine_ref.shape[-1]
    n = sums.shape[0] // 8
    y = at_ref[0]
    for at in range(0, depth, LANES):
        cols = slice(at, at + LANES)
        total = mine_ref[y, :, cols].astype(F32) + theirs_ref[y, :, cols].astype(F32)
        for got_ref in (a_ref, b_ref, c_ref):
            total = total + got_ref[:, cols] * jnp.exp2(got_ref[0:1, depth : depth + 1])
        sums[:, cols] = total

    def piece(k):
        step = jnp.where(at_ref[2] == 0, k, n - k)
        return pl.ds(pl.multiple_of(((at_ref[1] + step) % n) * 8, 8), 8)

    keep_ref[...] = sums[piece(0), :]
    near_ref[...] = sums[piece(1), :]
    scaled(sums.at[piece(2)], far_ref)
    scaled(sums.at[piece(3)], back_ref)


def add_y(at, mine, theirs, parts):
    _, rows, depth = mine.shape
    kept = jax.ShapeDtypeStruct((8, depth), F32)
    sent = jax.ShapeDtypeStruct((8, depth + 128), F32)
    return pl.pallas_call(
        add_y_kernel,
        in_specs=[SMEM] + [VMEM] * 5,
        out_specs=[VMEM] * 4,
        out_shape=[kept, kept, sent, sent],
        scratch_shapes=[pltpu.VMEM((rows, depth), F32)],
        compiler_params=PARAMS,
        name="add_y",
    )(at, mine, theirs, *parts)


def add_through_kernel(near_ref, got_ref, out_ref, total):
    total[...] = near_ref[...] + restored(got_ref, near_ref.shape[-1])
    scaled(total, out_ref)


def add_through(near, got):
    return pl.pallas_call(
        add_through_kernel,
        in_specs=[VMEM] * 2,
        out_specs=VMEM,
        out_shape=jax.ShapeDtypeStruct(got.shape, F32),
        scratch_shapes=[pltpu.VMEM(near.shape, F32)],
        compiler_params=PARAMS,
        name="add_through",
    )(near, got)


def turned(block, axis, distance):
    n = lax.axis_size(axis)
    pairs = []
    for i in range(n):
        pairs.append((2 * i, 2 * ((i + distance) % n)))
        pairs.append((2 * i + 1, 2 * ((i - distance) % n) + 1))
    return lax.ppermute(block.astype(jnp.float16), (axis, "core"), pairs).astype(F32)


def moments(mean, first, second):
    return 0.9 * first + 0.1 * mean, 0.95 * second + 0.05 * mean * mean


def adam_kernel(corr_ref, own_ref, far_ref, back_ref, master_ref, first_ref, second_ref, mean_ref, up_ref):
    depth = own_ref.shape[-1]
    total = own_ref[...] + (restored(far_ref, depth) + restored(back_ref, depth))
    mean_all = total * (1.0 / 32)
    mean_ref[...] = mean_all
    for layer in range(2):
        mean = mean_all[4 * layer : 4 * layer + 4]
        master = master_ref[layer]
        nf, ns = moments(mean, first_ref[layer], second_ref[layer])
        up_ref[layer] = master - 0.05 * (
            nf / corr_ref[0] / (jnp.sqrt(ns / corr_ref[1]) + 1e-08) + 0.1 * master
        )


def adam(corr, own, far, back, master, first, second):
    return pl.pallas_call(
        adam_kernel,
        in_specs=[SMEM] + [VMEM] * 6,
        out_specs=[VMEM] * 2,
        out_shape=[
            jax.ShapeDtypeStruct(own.shape, F32),
            jax.ShapeDtypeStruct(master.shape, F32),
        ],
        compiler_params=PARAMS,
        name="adam",
    )(corr, own, far, back, master, first, second)


def average_kernel(up_ref, partner_ref, rounded_ref):
    mean = [(up_ref[i] + partner_ref[i]) * 0.5 for i in range(2)]
    rounded_ref[...] = jnp.concatenate(mean, 0).astype(BF16)


def average(updated, partner):
    layers, rows, depth = updated.shape
    return pl.pallas_call(
        average_kernel,
        in_specs=[VMEM] * 2,
        out_specs=VMEM,
        out_shape=jax.ShapeDtypeStruct((layers * rows, depth), BF16),
        compiler_params=PARAMS,
        name="average",
    )(updated, partner)


def finish_kernel(mean_ref, first_ref, second_ref, up_ref, partner_ref, out_ref, nf_ref, ns_ref):
    for layer in range(2):
        mean = mean_ref[4 * layer : 4 * layer + 4, :]
        nf, ns = moments(mean, first_ref[layer], second_ref[layer])
        nf_ref[layer] = nf
        ns_ref[layer] = ns
        out_ref[layer] = (up_ref[layer] + partner_ref[layer]) * 0.5


def finish(mean, first, second, updated, partner):
    return pl.pallas_call(
        finish_kernel,
        in_specs=[VMEM] * 5,
        out_specs=[VMEM] * 3,
        out_shape=[jax.ShapeDtypeStruct(first.shape, F32)] * 3,
        compiler_params=PARAMS,
        name="finish",
    )(mean, first, second, updated, partner)


def join_kernel(core_ref, mine_ref, theirs_ref, out_ref, held, sems):
    first = core_ref[0] == 0
    n, _, per, depth = held.shape
    copies = []
    for k in range(n):
        rows = slice(k * per, (k + 1) * per)
        for at in range(0, depth, LANES):
            cols = slice(at, at + LANES)
            mine = mine_ref[rows, cols].astype(F32)
            theirs = theirs_ref[rows, cols].astype(F32)
            a = jnp.where(first, mine, theirs)
            b = jnp.where(first, theirs, mine)
            lows, highs = [], []
            for r in range(0, per, 8):
                low, high = low_high(a[r : r + 8], b[r : r + 8])
                lows.append(low)
                highs.append(high)
            held[k, 0, :, cols] = jnp.concatenate(lows, 0).astype(BF16)
            held[k, 1, :, cols] = jnp.concatenate(highs, 0).astype(BF16)
        copies.append(pltpu.make_async_copy(held.at[k], out_ref.at[:, rows, :], sems.at[k]))
        copies[k].start()
    for copy in copies:
        copy.wait()


def join_cores(mine, theirs, core):
    rows, depth = mine.shape
    steps = 4
    return pl.pallas_call(
        join_kernel,
        in_specs=[SMEM, VMEM, VMEM],
        out_specs=pl.BlockSpec(memory_space=pltpu.HBM),
        out_shape=jax.ShapeDtypeStruct((2, rows, depth), BF16),
        scratch_shapes=[
            pltpu.VMEM((steps, 2, rows // steps, depth), BF16),
            pltpu.SemaphoreType.DMA((steps,)),
        ],
        compiler_params=PARAMS,
        name="join_cores",
    )(core, mine, theirs)


def body(step, grads, master, first_moment, second_moment):
    t = step[0]
    power = (t + 1).astype(F32)
    corr = jnp.stack([1.0 - jnp.power(F32(0.9), power), 1.0 - jnp.power(F32(0.95), power)])
    y, z, core = (lax.axis_index(a).astype(jnp.int32)[None] for a in ZERO)
    at = jnp.concatenate([y, z, core])

    mine, theirs = split_cores(grads[0, 0, 0], core)
    theirs = shifted(theirs, "core", 1)
    theirs, at, corr = lax.optimization_barrier((theirs, at, corr))
    parts = [
        turned(add_pair(step, at, mine, theirs), "y", step) for step in (1, 3, 2)
    ]
    own, near, far, back = add_y(at, mine, theirs, parts)
    far = turned(far, "zhi", 1)
    back = turned(back, "zhi", -1)
    far = turned(add_through(near, far), "zhi", 1)
    mean, updated = adam(
        corr, own, back, far, master[0], first_moment[0], second_moment[0]
    )
    partner = lax.switch(
        t % 3, [lambda u, d=d: shifted(u, PEER, d) for d in (1, 2, 4)], updated
    )
    whole = average(updated, partner)
    whole = lax.all_gather(whole, "zhi", axis=0, tiled=True)
    whole = lax.all_gather(whole, "y", axis=0, tiled=True)
    whole, mean, updated, partner = lax.optimization_barrier((whole, mean, updated, partner))
    other = shifted(whole, "core", 1)
    averaged, new_first, new_second = finish(
        mean, first_moment[0], second_moment[0], updated, partner
    )
    whole = join_cores(whole, other, core)
    return (averaged[None], new_first[None], new_second[None], whole[None])


def solution(mesh):
    fine = Mesh(mesh.devices.reshape(4, 4, 4, 4, 2), PEER + ZERO)
    shard = P(PEER, None, ZERO, None)
    return jax.shard_map(
        body,
        mesh=fine,
        in_specs=(P(), P(PEER, ZERO, None, None, None, None), shard, shard, shard),
        out_specs=(shard, shard, shard, P(PEER, None, None, None)),
        check_vma=False,
    )
```

```python
import jax
import jax.numpy as jnp
from jax import lax
from jax.experimental import pallas as pl
from jax.experimental.pallas import tpu as pltpu
from jax.sharding import Mesh, PartitionSpec as P

PEER = ("zlo", "x")
ZERO = ("y", "zhi", "core")
F32 = jnp.float32
BF16 = jnp.bfloat16
VMEM = pl.BlockSpec(memory_space=pltpu.VMEM)
SMEM = pl.BlockSpec(memory_space=pltpu.SMEM)
LANES = 512
PARAMS = pltpu.CompilerParams(vmem_limit_bytes=32 * 2**20)


def shifted(block, axis, distance):
    n = lax.axis_size(axis)
    return lax.ppermute(block, axis, [(i, (i + distance) % n) for i in range(n)])


def low_high(a, b):
    row = lax.broadcasted_iota(jnp.int32, a.shape, 0)
    low = jnp.where(row < 4, a, pltpu.roll(b, 4, 0))
    high = jnp.where(row < 4, pltpu.roll(a, 4, 0), b)
    return low, high


def split_kernel(core_ref, grads_ref, mine_ref, theirs_ref, held, sems):
    first = core_ref[0] == 0
    n, _, per, depth = held.shape
    copies = [
        pltpu.make_async_copy(
            grads_ref.at[:, k * per : (k + 1) * per, :], held.at[k], sems.at[k]
        )
        for k in range(n)
    ]
    for copy in copies:
        copy.start()
    for k, copy in enumerate(copies):
        copy.wait()
        for at in range(0, depth, LANES):
            cols = slice(at, at + LANES)
            a = held[k, 0, :, cols].astype(F32)
            b = held[k, 1, :, cols].astype(F32)
            mine, theirs = [], []
            for r in range(0, per, 8):
                low, high = low_high(a[r : r + 8], b[r : r + 8])
                mine.append(jnp.where(first, low, high))
                theirs.append(jnp.where(first, high, low))
            mine_ref[k, :, cols] = jnp.concatenate(mine, 0).astype(BF16)
            theirs_ref[k, :, cols] = jnp.concatenate(theirs, 0).astype(BF16)


def split_cores(grads, core):
    layers, rows, depth = grads.shape
    ny = lax.axis_size("y")
    per = rows // ny
    out = jax.ShapeDtypeStruct((ny, per, depth), BF16)
    return pl.pallas_call(
        split_kernel,
        in_specs=[SMEM, pl.BlockSpec(memory_space=pltpu.HBM)],
        out_specs=[VMEM] * 2,
        out_shape=(out, out),
        scratch_shapes=[
            pltpu.VMEM((ny, layers, per, depth), BF16),
            pltpu.SemaphoreType.DMA((ny,)),
        ],
        compiler_params=pltpu.CompilerParams(vmem_limit_bytes=52 * 2**20),
        name="split_cores",
    )(core, grads)


def scale_of(largest):
    exponent = 14.0 - jnp.floor(jnp.log2(jnp.maximum(largest, 1e-30)))
    return jnp.exp2(exponent), -exponent


def add_pair_kernel(at_ref, mine_ref, theirs_ref, near_ref, far_ref, back_ref, sums):
    n, per, depth = mine_ref.shape
    largest = jnp.zeros((8, LANES), F32)
    for k in range(n):
        for at in range(0, depth, LANES):
            cols = slice(at, at + LANES)
            total = mine_ref[k, :, cols].astype(F32) + theirs_ref[k, :, cols].astype(F32)
            sums[k * per : (k + 1) * per, cols] = total
            for r in range(0, per, 8):
                largest = jnp.maximum(largest, jnp.abs(total[r : r + 8]))
    scale, back = scale_of(jnp.max(largest, axis=(0, 1), keepdims=True))

    def piece(k):
        step = jnp.where(at_ref[2] == 0, k, n - k)
        return pl.ds(pl.multiple_of(((at_ref[0] + step) % n) * per, per), per)

    for k, out_ref in ((1, near_ref), (2, far_ref), (3, back_ref)):
        rows = piece(k)
        for at in range(0, depth, LANES):
            cols = slice(at, at + LANES)
            out_ref[:, cols] = sums[rows, cols] * scale
        out_ref[:, depth:] = jnp.broadcast_to(back, (per, out_ref.shape[-1] - depth))


def add_pair(at, mine, theirs):
    n, rows, depth = mine.shape
    return pl.pallas_call(
        add_pair_kernel,
        in_specs=[SMEM, VMEM, VMEM],
        out_specs=[VMEM] * 3,
        out_shape=[jax.ShapeDtypeStruct((rows, depth + 128), F32)] * 3,
        scratch_shapes=[pltpu.VMEM((n * rows, depth), F32)],
        compiler_params=PARAMS,
        name="add_pair",
    )(at, mine, theirs)


def scaled(block_ref, out_ref):
    depth = block_ref.shape[-1]
    largest = jnp.zeros((8, LANES), F32)
    for at in range(0, depth, LANES):
        largest = jnp.maximum(largest, jnp.abs(block_ref[:, at : at + LANES]))
    scale, back = scale_of(jnp.max(largest, axis=(0, 1), keepdims=True))
    out_ref[:, :depth] = block_ref[...] * scale
    out_ref[:, depth:] = jnp.broadcast_to(back, (8, out_ref.shape[-1] - depth))


def restored(got_ref, depth):
    return got_ref[:, :depth] * jnp.exp2(got_ref[0:1, depth : depth + 1])


def add_y_kernel(at_ref, mine_ref, theirs_ref, a_ref, b_ref, c_ref, keep_ref, near_ref, far_ref, back_ref, sums):
    depth = mine_ref.shape[-1]
    n = sums.shape[0] // 8
    y = at_ref[0]
    for at in range(0, depth, LANES):
        cols = slice(at, at + LANES)
        total = mine_ref[y, :, cols].astype(F32) + theirs_ref[y, :, cols].astype(F32)
        for got_ref in (a_ref, b_ref, c_ref):
            total = total + got_ref[:, cols] * jnp.exp2(got_ref[0:1, depth : depth + 1])
        sums[:, cols] = total

    def piece(k):
        step = jnp.where(at_ref[2] == 0, k, n - k)
        return pl.ds(pl.multiple_of(((at_ref[1] + step) % n) * 8, 8), 8)

    keep_ref[...] = sums[piece(0), :]
    near_ref[...] = sums[piece(1), :]
    scaled(sums.at[piece(2)], far_ref)
    scaled(sums.at[piece(3)], back_ref)


def add_y(at, mine, theirs, parts):
    _, rows, depth = mine.shape
    kept = jax.ShapeDtypeStruct((8, depth), F32)
    sent = jax.ShapeDtypeStruct((8, depth + 128), F32)
    return pl.pallas_call(
        add_y_kernel,
        in_specs=[SMEM] + [VMEM] * 5,
        out_specs=[VMEM] * 4,
        out_shape=[kept, kept, sent, sent],
        scratch_shapes=[pltpu.VMEM((rows, depth), F32)],
        compiler_params=PARAMS,
        name="add_y",
    )(at, mine, theirs, *parts)


def add_through_kernel(near_ref, got_ref, out_ref, total):
    total[...] = near_ref[...] + restored(got_ref, near_ref.shape[-1])
    scaled(total, out_ref)


def add_through(near, got):
    return pl.pallas_call(
        add_through_kernel,
        in_specs=[VMEM] * 2,
        out_specs=VMEM,
        out_shape=jax.ShapeDtypeStruct(got.shape, F32),
        scratch_shapes=[pltpu.VMEM(near.shape, F32)],
        compiler_params=PARAMS,
        name="add_through",
    )(near, got)


def turned(block, axis, distance):
    n = lax.axis_size(axis)
    pairs = []
    for i in range(n):
        pairs.append((2 * i, 2 * ((i + distance) % n)))
        pairs.append((2 * i + 1, 2 * ((i - distance) % n) + 1))
    return lax.ppermute(block.astype(jnp.float16), (axis, "core"), pairs).astype(F32)


def moments(mean, first, second):
    return 0.9 * first + 0.1 * mean, 0.95 * second + 0.05 * mean * mean


def adam_kernel(corr_ref, own_ref, far_ref, back_ref, master_ref, first_ref, second_ref, mean_ref, up_ref):
    depth = own_ref.shape[-1]
    total = own_ref[...] + (restored(far_ref, depth) + restored(back_ref, depth))
    mean_all = total * (1.0 / 32)
    mean_ref[...] = mean_all
    for layer in range(2):
        mean = mean_all[4 * layer : 4 * layer + 4]
        master = master_ref[layer]
        nf, ns = moments(mean, first_ref[layer], second_ref[layer])
        up_ref[layer] = master - 0.05 * (
            nf / corr_ref[0] / (jnp.sqrt(ns / corr_ref[1]) + 1e-08) + 0.1 * master
        )


def adam(corr, own, far, back, master, first, second):
    return pl.pallas_call(
        adam_kernel,
        in_specs=[SMEM] + [VMEM] * 6,
        out_specs=[VMEM] * 2,
        out_shape=[
            jax.ShapeDtypeStruct(own.shape, F32),
            jax.ShapeDtypeStruct(master.shape, F32),
        ],
        compiler_params=PARAMS,
        name="adam",
    )(corr, own, far, back, master, first, second)


def average_kernel(up_ref, partner_ref, rounded_ref):
    mean = [(up_ref[i] + partner_ref[i]) * 0.5 for i in range(2)]
    rounded_ref[...] = jnp.concatenate(mean, 0).astype(BF16)


def average(updated, partner):
    layers, rows, depth = updated.shape
    return pl.pallas_call(
        average_kernel,
        in_specs=[VMEM] * 2,
        out_specs=VMEM,
        out_shape=jax.ShapeDtypeStruct((layers * rows, depth), BF16),
        compiler_params=PARAMS,
        name="average",
    )(updated, partner)


def finish_kernel(mean_ref, first_ref, second_ref, up_ref, partner_ref, out_ref, nf_ref, ns_ref):
    for layer in range(2):
        mean = mean_ref[4 * layer : 4 * layer + 4, :]
        nf, ns = moments(mean, first_ref[layer], second_ref[layer])
        nf_ref[layer] = nf
        ns_ref[layer] = ns
        out_ref[layer] = (up_ref[layer] + partner_ref[layer]) * 0.5


def finish(mean, first, second, updated, partner):
    return pl.pallas_call(
        finish_kernel,
        in_specs=[VMEM] * 5,
        out_specs=[VMEM] * 3,
        out_shape=[jax.ShapeDtypeStruct(first.shape, F32)] * 3,
        compiler_params=PARAMS,
        name="finish",
    )(mean, first, second, updated, partner)


def join_kernel(core_ref, mine_ref, theirs_ref, out_ref, held, sems):
    first = core_ref[0] == 0
    n, _, per, depth = held.shape
    copies = []
    for k in range(n):
        rows = slice(k * per, (k + 1) * per)
        for at in range(0, depth, LANES):
            cols = slice(at, at + LANES)
            mine = mine_ref[rows, cols].astype(F32)
            theirs = theirs_ref[rows, cols].astype(F32)
            a = jnp.where(first, mine, theirs)
            b = jnp.where(first, theirs, mine)
            lows, highs = [], []
            for r in range(0, per, 8):
                low, high = low_high(a[r : r + 8], b[r : r + 8])
                lows.append(low)
                highs.append(high)
            held[k, 0, :, cols] = jnp.concatenate(lows, 0).astype(BF16)
            held[k, 1, :, cols] = jnp.concatenate(highs, 0).astype(BF16)
        copies.append(pltpu.make_async_copy(held.at[k], out_ref.at[:, rows, :], sems.at[k]))
        copies[k].start()
    for copy in copies:
        copy.wait()


def join_cores(mine, theirs, core):
    rows, depth = mine.shape
    steps = 4
    return pl.pallas_call(
        join_kernel,
        in_specs=[SMEM, VMEM, VMEM],
        out_specs=pl.BlockSpec(memory_space=pltpu.HBM),
        out_shape=jax.ShapeDtypeStruct((2, rows, depth), BF16),
        scratch_shapes=[
            pltpu.VMEM((steps, 2, rows // steps, depth), BF16),
            pltpu.SemaphoreType.DMA((steps,)),
        ],
        compiler_params=PARAMS,
        name="join_cores",
    )(core, mine, theirs)


def body(step, grads, master, first_moment, second_moment):
    t = step[0]
    power = (t + 1).astype(F32)
    corr = jnp.stack([1.0 - jnp.power(F32(0.9), power), 1.0 - jnp.power(F32(0.95), power)])
    y, z, core = (lax.axis_index(a).astype(jnp.int32)[None] for a in ZERO)
    at = jnp.concatenate([y, z, core])

    mine, theirs = split_cores(grads[0, 0, 0], core)
    theirs = shifted(theirs, "core", 1)
    theirs, at, corr = lax.optimization_barrier((theirs, at, corr))
    near, far, back = add_pair(at, mine, theirs)
    parts = [turned(near, "y", 1), turned(back, "y", -1), turned(far, "y", 2)]
    own, near, far, back = add_y(at, mine, theirs, parts)
    far = turned(far, "zhi", 1)
    back = turned(back, "zhi", -1)
    far = turned(add_through(near, far), "zhi", 1)
    mean, updated = adam(
        corr, own, back, far, master[0], first_moment[0], second_moment[0]
    )
    partner = lax.switch(
        t % 3, [lambda u, d=d: shifted(u, PEER, d) for d in (1, 2, 4)], updated
    )
    whole = average(updated, partner)
    whole = lax.all_gather(whole, "zhi", axis=0, tiled=True)
    whole = lax.all_gather(whole, "y", axis=0, tiled=True)
    whole, mean, updated, partner = lax.optimization_barrier((whole, mean, updated, partner))
    other = shifted(whole, "core", 1)
    averaged, new_first, new_second = finish(
        mean, first_moment[0], second_moment[0], updated, partner
    )
    whole = join_cores(whole, other, core)
    return (averaged[None], new_first[None], new_second[None], whole[None])


def solution(mesh):
    fine = Mesh(mesh.devices.reshape(4, 4, 4, 4, 2), PEER + ZERO)
    shard = P(PEER, None, ZERO, None)
    return jax.shard_map(
        body,
        mesh=fine,
        in_specs=(P(), P(PEER, ZERO, None, None, None, None), shard, shard, shard),
        out_specs=(shard, shard, shard, P(PEER, None, None, None)),
        check_vma=False,
    )
```
